128 devices in a mesh: leaf: 32 (over y, x, core), mp: 4 (over z).
Axes of the slice: x: 4, y: 4, z: 4, core: 2. Of those that a mesh axis runs over, the one named last changes fastest.
Arguments:
- tokens: bfloat16 [32768, 4608], P('leaf', 'mp'), may hold values from -6 to 6
- norm_gain: bfloat16 [4608], replicated, may hold values from 0.099609375 to 1.8984375
- w_query: bfloat16 [4608, 2048], P(None, 'mp'), may hold values from -0.25 to 0.25
- w_key: bfloat16 [4608, 1024], P(None, 'mp'), may hold values from -0.09375 to 0.09375
- w_value: bfloat16 [4608, 1024], P(None, 'mp'), may hold values from -0.09375 to 0.09375
- gen_node: int32 [512], P('leaf'), may hold values from 0 to 511, as said below
- partition: int32 [32], replicated, may hold values from 1 to 31, as said below
- parent: int32 [512], replicated, may hold values from 0 to 511, as said below
- block_mask: int32 [512, 512], replicated, may hold values from 0 to 1, as said below
Outputs:
- attended: bfloat16 [63488, 2048], P('leaf', 'mp')
The draws below stay inside these ranges and needn't reach their ends.
Inputs may be any that keep to these rules, and one draw needn't show every extreme that they name: `gen_node`: A permutation of the nodes. At most 1 nodes of one device's generation slots belong to one subtree owner. `partition`: the counts sum to 512; owner d holds the consecutive nodes that start at the sum of the earlier counts. Node 0 is the root and its own parent; every other node's parent has a smaller number, and the numbers follow a depth-first order, so that a subtree's nodes are consecutive. block_mask[i, j] is 1 only where j is i or an ancestor of i; the diagonal is 1; a row holds at most 8 ones; at most 2 nodes of one owner are seen by nodes of other owners.
All inputs are finite; a program needn't handle non-finite values.
Results may differ from the reference program's by a relative error of at most 0.012.
The reference program's roundings to bfloat16 on the way count: a program that leaves them out, or rounds other values in their place, can miss the bound.
Values may be sent and summed in bfloat16 or wider, within the bound.
A program may use at most 128 MiB of HBM per device.

```python
import math
import jax
import jax.numpy as jnp
from jax import lax

D = 4608
QH = 16
KH = 8
HD = 128
NODE_TOK = 64
NODE_DEV = 16
TRUNK = 2
WIN = 5
NODES_ALL = 512
OWNERS = 32
CAP = 31
ANC = 8
EXPORT = 2


def build_forest(key):
    count_key = jax.random.fold_in(key, 11)
    walk_key = jax.random.fold_in(key, 12)
    window_key = jax.random.fold_in(key, 13)
    order_key = jax.random.fold_in(key, 14)
    shuffle_key = jax.random.fold_in(key, 15)
    pick_key = jax.random.fold_in(key, 16)
    halves = OWNERS // 2
    devices = jax.random.permutation(count_key, OWNERS).astype(jnp.int32)
    upper_side = devices[:halves]
    lower_side = devices[halves:]
    swapped = lower_side == 0
    upper_new = jnp.where(swapped, lower_side, upper_side)
    lower_new = jnp.where(swapped, upper_side, lower_side)
    surplus = jax.random.randint(jax.random.fold_in(count_key, 1), (halves,), 0, NODE_DEV).astype(jnp.int32)
    chosen = jax.random.randint(pick_key, (), 0, halves)
    surplus = jnp.where(jnp.arange(halves) == chosen, NODE_DEV - 1, surplus).astype(jnp.int32)
    counts = jnp.zeros((OWNERS,), jnp.int32).at[upper_new].set(NODE_DEV + surplus).at[lower_new].set(NODE_DEV - surplus)
    backtrack = jax.random.randint(walk_key, (NODES_ALL,), 0, 3).astype(jnp.int32)

    def advance(node_index, state):
        path_stack, level_now, parents, depths = state
        parent_level = jnp.where(node_index < ANC, level_now, jnp.maximum(level_now - backtrack[node_index], TRUNK - 1))
        parents = parents.at[node_index].set(path_stack[parent_level])
        path_stack = path_stack.at[parent_level + 1].set(node_index)
        depths = depths.at[node_index].set(parent_level + 1)
        return (path_stack, parent_level + 1, parents, depths)
    start_state = (jnp.zeros((NODES_ALL + 1,), jnp.int32), jnp.int32(0), jnp.zeros((NODES_ALL,), jnp.int32), jnp.zeros((NODES_ALL,), jnp.int32))
    path_stack, level_now, parents, depths = lax.fori_loop(1, NODES_ALL, advance, start_state)
    node_ids = jnp.arange(NODES_ALL, dtype=jnp.int32)

    def climb(rounds, state):
        pointer, ancestors = state
        pointer = parents[pointer]
        ancestors = ancestors | (pointer[:, None] == node_ids[None, :])
        return (pointer, ancestors)
    pointer, ancestors = lax.fori_loop(0, NODES_ALL, climb, (node_ids, jnp.zeros((NODES_ALL, NODES_ALL), bool)))
    diagonal = node_ids[:, None] == node_ids[None, :]
    ancestors = ancestors & ~diagonal
    window_len = jax.random.randint(window_key, (NODES_ALL,), 1, WIN + 1).astype(jnp.int32)
    window_len = jnp.where(node_ids == ANC - 1, WIN, window_len)
    in_window = depths[:, None] - depths[None, :] <= window_len[:, None]
    in_trunk = depths[None, :] < TRUNK
    visible = diagonal | ancestors & (in_trunk | in_window)
    range_end = jnp.cumsum(counts).astype(jnp.int32)
    starts = (range_end - counts).astype(jnp.int32)
    owners = jnp.sum((node_ids[:, None] >= range_end[None, :]).astype(jnp.int32), axis=1).astype(jnp.int32)
    foreign = owners[:, None] != owners[None, :]
    exported = jnp.any(visible & foreign, axis=0).astype(jnp.int32)
    running = jnp.cumsum(exported).astype(jnp.int32)
    before = running - exported
    export_rank = before - before[starts[owners]]
    kept = export_rank < EXPORT
    block_mask = (visible & (~foreign | kept[None, :])).astype(jnp.int32)
    sources = jax.random.permutation(order_key, OWNERS).astype(jnp.int32)
    source_of = sources[node_ids % OWNERS]
    rank_in = node_ids // OWNERS

    def shuffle_one(sub_key):
        return jax.random.permutation(sub_key, NODE_DEV).astype(jnp.int32)
    shuffles = jax.vmap(shuffle_one)(jax.random.split(shuffle_key, OWNERS))
    slot_of = shuffles[source_of, rank_in]
    placed = jnp.zeros((NODES_ALL,), jnp.int32).at[source_of * NODE_DEV + slot_of].set(node_ids)
    return (parents, block_mask, counts, placed)


def draw_parent(key, part):
    forest = build_forest(key)
    return forest[0]


def draw_block_mask(key, part):
    forest = build_forest(key)
    return forest[1]


def draw_partition(key, part):
    forest = build_forest(key)
    return forest[2]


def draw_gen_node(key, part):
    forest = build_forest(key)
    return forest[3]


def block_scale(key, dims, pieces, low, largest):
    def one(axis_at, parts):
        draws = jax.random.uniform(jax.random.fold_in(jax.random.fold_in(key, 6), axis_at), (parts,), jnp.float32, low / len(pieces), largest / len(pieces))
        return jnp.repeat(jnp.exp(draws), dims[axis_at] // parts).reshape((-1,) + (1,) * (len(dims) - axis_at - 1))

    gain = one(*pieces[0])
    for cut in pieces[1:]:
        gain = gain * one(*cut)
    return gain


def gaussian(key, shape, scale, most, cuts=(), held_as=jnp.bfloat16):
    level = block_scale(key, shape, cuts, -0.22, 0.18) if cuts else 1.0
    values = jax.random.normal(key, shape, jnp.float32) * scale * level
    return jnp.minimum(jnp.maximum(values, -most), most).astype(held_as)


def setup_inputs(seed: int = 0) -> dict:
    keys = jax.random.split(jax.random.key(seed), 10)
    tokens = gaussian(keys[0], (NODES_ALL * NODE_TOK, D), 1.0, 6.0, ((0, 32), (1, 4)))
    norm_gain = jnp.clip(1.0 + 0.18 * jax.random.normal(keys[1], (D,), jnp.float32), 0.099609375, 1.8984375).astype(jnp.bfloat16)
    w_query = gaussian(keys[2], (D, QH * HD), (D // 9) ** -0.5, 0.25, ((1, 4),))
    w_key = gaussian(keys[3], (D, KH * HD), D ** -0.5, 0.09375, ((1, 4),))
    w_value = gaussian(keys[4], (D, KH * HD), D ** -0.5, 0.09375, ((1, 4),))
    gen_node = draw_gen_node(jax.random.fold_in(keys[9], 71), 0)
    partition = draw_partition(jax.random.fold_in(keys[9], 71), 0)
    parent = draw_parent(jax.random.fold_in(keys[9], 71), 0)
    block_mask = draw_block_mask(jax.random.fold_in(keys[9], 71), 0)
    return {"tokens": tokens, "norm_gain": norm_gain, "w_query": w_query, "w_key": w_key, "w_value": w_value, "gen_node": gen_node, "partition": partition, "parent": parent, "block_mask": block_mask}


norm_epsilon = 1e-06
soft_cap = 50.0
query_scale = 144.0 ** (-0.5)
rope_base = 10000.0

def node_depth(parent):
    node_total = parent.shape[0]
    pointer = parent
    distance = (pointer != jnp.arange(node_total, dtype=jnp.int32)).astype(jnp.int32)
    for rounds in range(node_total.bit_length()):
        distance = (distance + distance[pointer]).astype(jnp.int32)
        pointer = pointer[pointer]
    return distance

def rotate_pairs(values, position):
    half_dim = values.shape[-1] // 2
    inverse_freq = jnp.exp(jnp.arange(half_dim, dtype=jnp.float32) * (-2.0 * math.log(rope_base) / values.shape[-1]))
    angles = position[..., None, None] * inverse_freq
    cosine = jnp.cos(angles)
    sine_part = jnp.sin(angles)
    first_half = values[..., :half_dim]
    second = values[..., half_dim:]
    return jnp.concatenate([first_half * cosine - second * sine_part, second * cosine + first_half * sine_part], axis=-1)

def select_blocks(visible, width):
    ranks = (jnp.cumsum(visible, axis=1) - 1).astype(jnp.int32)
    column = jnp.arange(visible.shape[1], dtype=jnp.int32)
    target = jnp.arange(width, dtype=jnp.int32)
    matched = visible[:, None, :] * (ranks[:, None, :] == target[None, :, None]).astype(jnp.int32)
    picked = lax.optimization_barrier(jnp.sum(matched * column[None, None, :], axis=2)).astype(jnp.int32)
    usable = lax.optimization_barrier(jnp.sum(matched, axis=2)).astype(jnp.int32)
    return (picked, usable)

def attend_node(queries, key_rows, values, key_node, usable, self_node):
    scores = jnp.einsum('qhgd,akhd->hgqak', queries.astype(jnp.float32), key_rows.astype(jnp.float32)) * query_scale
    capped = soft_cap * jnp.tanh(scores / soft_cap)
    node_tok = queries.shape[0]
    tok_ids = jnp.arange(node_tok, dtype=jnp.int32)
    causal = tok_ids[None, :] <= tok_ids[:, None]
    is_self = key_node == self_node
    allowed = (usable > 0)[None, :, None] & ((~is_self)[None, :, None] | causal[:, None, :])
    probs = jnp.where(allowed[None, None], jnp.exp(capped), 0.0)
    totals = lax.optimization_barrier(jnp.sum(probs, axis=(3, 4)))
    numer = jnp.einsum('hgqak,akhd->qhgd', probs.astype(jnp.bfloat16).astype(jnp.float32), values.astype(jnp.float32))
    return (numer, jnp.transpose(totals, (2, 0, 1)))

def reference(tokens, norm_gain, w_query, w_key, w_value, gen_node, partition, parent, block_mask):
    node_total = parent.shape[0]
    node_tok = tokens.shape[0] // node_total
    width = tokens.shape[1]
    blocks = tokens.reshape(node_total, node_tok, width)
    by_node = jnp.zeros_like(blocks).at[gen_node].set(blocks)
    flat_rows = by_node.reshape(node_total * node_tok, width)
    wide = flat_rows.astype(jnp.float32)
    scaled = (wide * norm_gain.astype(jnp.float32)[None, :]).astype(jnp.bfloat16)
    row_scale = lax.rsqrt(lax.optimization_barrier(jnp.sum(wide * wide, axis=1)) / width + norm_epsilon)[:, None]
    depths = node_depth(parent)
    position = (depths[:, None] * node_tok + jnp.arange(node_tok, dtype=jnp.int32)[None, :]).astype(jnp.float32)
    query_heads = w_query.shape[1] // HD
    key_heads = w_key.shape[1] // HD
    groups = query_heads // key_heads
    query_raw = jnp.dot(scaled, w_query, preferred_element_type=jnp.float32) * row_scale
    queries = rotate_pairs(query_raw.reshape(node_total, node_tok, query_heads, HD), position).astype(jnp.bfloat16)
    key_raw = jnp.dot(scaled, w_key, preferred_element_type=jnp.float32) * row_scale
    key_rows = rotate_pairs(key_raw.reshape(node_total, node_tok, key_heads, HD), position).astype(jnp.bfloat16)
    value_raw = jnp.dot(scaled, w_value, preferred_element_type=jnp.float32) * row_scale
    values = value_raw.reshape(node_total, node_tok, key_heads, HD).astype(jnp.bfloat16)
    picked, usable = select_blocks(block_mask, ANC)

    def one_node(node_index):
        chosen = picked[node_index]
        numer, totals = attend_node(queries[node_index].reshape(node_tok, key_heads, groups, HD), key_rows[chosen], values[chosen], chosen, usable[node_index], node_index)
        return (numer / totals[..., None]).astype(jnp.bfloat16).reshape(node_tok, query_heads * HD)
    node_out = lax.map(one_node, jnp.arange(node_total, dtype=jnp.int32))
    owner_count = partition.shape[0]
    range_end = jnp.cumsum(partition).astype(jnp.int32)
    starts = (range_end - partition).astype(jnp.int32)
    node_ids = jnp.arange(node_total, dtype=jnp.int32)
    owners = lax.optimization_barrier(jnp.sum((node_ids[:, None] >= range_end[None, :]).astype(jnp.int32), axis=1)).astype(jnp.int32)
    slot_of = (owners * CAP + node_ids - starts[owners]).astype(jnp.int32)
    placed = jnp.zeros((owner_count * CAP, node_tok, query_heads * HD), jnp.bfloat16).at[slot_of].set(node_out)
    return placed.reshape(owner_count * CAP * node_tok, query_heads * HD)
```

```python
import functools
import math

import jax
import jax.numpy as jnp
from jax import lax
from jax.experimental import pallas as pl
from jax.experimental.pallas import tpu as pltpu
from jax.sharding import PartitionSpec as P

HD = 128
CAP = 31
ANC = 8
EXPORT = 2
CHUNKS = 4
NODE_TOK = 64
TOK = NODE_TOK // CHUNKS

norm_epsilon = 1e-06
soft_cap = 50.0
query_scale = 144.0 ** (-0.5)
rope_base = 10000.0

MESH = pl.DeviceIdType.MESH


def project_kernel(
    leafs, nodes, width, q_cols, k_cols,
    gen_ref, part_ref, parent_ref, mask_ref, gain_ref, freq_ref, tok_ref, wq_ref, wk_ref, wv_ref,
    qkv_ref, far_ref, table_ref,
    pieces, weights, scaled, acc, squares, angle_cos, angle_sin, made, send, recv, far,
    ids_out, ids_in, export_src,
    depth_sm, index_sm, start_sm, end_sm,
    load_sem, own_sem, full_send, full_recv, half_send, half_recv, ids_send, ids_recv,
    slot_send, slot_recv, slot_own, qkv_sem, far_sem,
    x_send, x_recv, y_send, y_recv, core_send, core_recv,
):
    me = lax.axis_index("leaf")
    z = lax.axis_index("mp")
    mp = 4
    right, left = lax.rem(z + 1, mp), lax.rem(z + 3, mp)
    opposite = lax.rem(z + 2, mp)
    feat = width // mp
    rows = nodes * TOK
    cols = q_cols + 2 * k_cols
    half = nodes // 2
    node_total = parent_ref.shape[0]
    core = lax.rem(me, 2)
    chip = lax.div(me, 2)
    cx = lax.rem(chip, 4)
    cy = lax.div(chip, 4)

    loads = [
        pltpu.make_async_copy(wq_ref, weights.at[:, :, pl.ds(0, q_cols)], load_sem.at[0]),
        pltpu.make_async_copy(wk_ref, weights.at[:, :, pl.ds(q_cols, k_cols)], load_sem.at[1]),
        pltpu.make_async_copy(wv_ref, weights.at[:, :, pl.ds(q_cols + k_cols, k_cols)], load_sem.at[2]),
    ]

    def own_load(c):
        return pltpu.make_async_copy(
            tok_ref.at[:, pl.ds(pl.multiple_of(c * TOK, TOK), TOK), :], pieces.at[z, c], own_sem.at[c]
        )

    barrier = pltpu.get_barrier_semaphore()

    def greet(o, carry):
        peer = lax.rem(me + o, leafs)
        pl.semaphore_signal(barrier, inc=1, device_id=(peer, z), device_id_type=MESH)
        return carry

    lax.fori_loop(1, leafs, greet, 0)
    pl.semaphore_signal(barrier, inc=1, device_id=(me, right), device_id_type=MESH)
    pl.semaphore_signal(barrier, inc=1, device_id=(me, left), device_id_type=MESH)
    for c in range(CHUNKS):
        own_load(c).start()
    for load in loads:
        load.start()
    pl.semaphore_wait(barrier, leafs + 1)

    def full(side, c):
        return pltpu.make_async_remote_copy(
            src_ref=pieces.at[z, c],
            dst_ref=pieces.at[z, c],
            send_sem=full_send.at[side, c],
            recv_sem=full_recv.at[side, c],
            device_id=(me, right if side == 0 else left),
            device_id_type=MESH,
        )

    def full_arrival(side, c):
        source = left if side == 0 else right
        return pltpu.make_async_remote_copy(
            src_ref=pieces.at[source, c],
            dst_ref=pieces.at[source, c],
            send_sem=full_send.at[side, c],
            recv_sem=full_recv.at[side, c],
            device_id=(me, right if side == 0 else left),
            device_id_type=MESH,
        )

    def forward(side, c):
        source = left if side == 0 else right
        part = pieces.at[source, c, pl.ds(side * half, half)]
        return pltpu.make_async_remote_copy(
            src_ref=part,
            dst_ref=part,
            send_sem=half_send.at[side, c],
            recv_sem=half_recv.at[side, c],
            device_id=(me, right if side == 0 else left),
            device_id_type=MESH,
        )

    def forward_arrival(side, c):
        part = pieces.at[opposite, c, pl.ds(side * half, half)]
        return pltpu.make_async_remote_copy(
            src_ref=part,
            dst_ref=part,
            send_sem=half_send.at[side, c],
            recv_sem=half_recv.at[side, c],
            device_id=(me, right if side == 0 else left),
            device_id_type=MESH,
        )

    for c in range(2):
        own_load(c).wait()
        full(0, c).start()
        full(1, c).start()
    for c in range(2, CHUNKS):
        own_load(c).wait()

    def ranges(d, first):
        last = first + part_ref[d]
        start_sm[d] = first
        end_sm[d] = last
        found = jnp.int32(0)
        for b in range(nodes):
            node = gen_ref[b]
            found = found + jnp.where((node >= first) & (node < last), b + 1, 0)
        index_sm[d] = jnp.maximum(found - 1, 0)
        ids_out[d] = jnp.full((8, 128), jnp.where(found > 0, gen_ref[jnp.maximum(found - 1, 0)], -1), jnp.int32)
        return last

    lax.fori_loop(0, leafs, ranges, jnp.int32(0))

    def ids_copy(o):
        peer = lax.rem(me + o, leafs)
        return pltpu.make_async_remote_copy(
            src_ref=ids_out.at[peer],
            dst_ref=ids_in.at[me],
            send_sem=ids_send,
            recv_sem=ids_recv,
            device_id=(peer, z),
            device_id_type=MESH,
        )

    lax.fori_loop(1, leafs, lambda o, carry: (ids_copy(o).start(), carry)[1], 0)
    ids_in[me] = ids_out[me]

    depth_sm[0] = jnp.int32(0)

    def deeper(n, carry):
        depth_sm[n] = depth_sm[parent_ref[n]] + 1
        return carry

    lax.fori_loop(1, node_total, deeper, 0)

    token_row = lax.broadcasted_iota(jnp.int32, (TOK, HD), 0)
    sign = jnp.where(lax.broadcasted_iota(jnp.int32, (rows, HD), 1) < HD // 2, -1.0, 1.0)

    def tables(c, carry):
        def one_node(b, carry2):
            position = depth_sm[gen_ref[b]] * NODE_TOK + c * TOK + token_row
            at = pl.ds(pl.multiple_of(b * TOK, TOK), TOK)
            angle_cos[c, at, :] = position.astype(jnp.float32) * freq_ref[...]
            return carry2

        lax.fori_loop(0, nodes, one_node, 0)
        angles = angle_cos[c]
        angle_sin[c] = jnp.sin(angles) * sign
        angle_cos[c] = jnp.cos(angles)
        return carry

    lax.fori_loop(0, CHUNKS, tables, 0)

    lane8 = lax.broadcasted_iota(jnp.int32, (8, node_total), 1)

    def spans(step, carry):
        d = leafs - 1 - step
        end_of, start_of, owner = carry
        inside = lane8 < end_sm[d]
        return (
            jnp.where(inside, end_sm[d], end_of),
            jnp.where(inside, start_sm[d], start_of),
            jnp.where(inside, d, owner),
        )

    blank = jnp.zeros((8, node_total), jnp.int32)
    end_of, start_of, owner = lax.fori_loop(0, leafs, spans, (blank, blank, blank))
    my_start = start_sm[me]
    row_id = lax.broadcasted_iota(jnp.int32, (node_total, node_total), 0)
    col_id = lax.broadcasted_iota(jnp.int32, (node_total, node_total), 1)
    mask = mask_ref[...]
    foreign = (mask > 0) & (row_id >= end_of[0:1, :])
    seen = jnp.max(jnp.where(foreign, 1.0, 0.0), axis=0, keepdims=True)
    earlier = jnp.where((row_id < col_id) & (row_id >= start_of[0:1, :]), 1.0, 0.0).astype(jnp.bfloat16)
    seen8 = jnp.broadcast_to(seen, (8, node_total))
    rank8 = jnp.dot(seen8.astype(jnp.bfloat16), earlier, preferred_element_type=jnp.float32)
    owner_f = owner.astype(jnp.float32)
    core_f = lax.rem(owner, 2).astype(jnp.float32)
    chip_f = lax.div(owner, 2).astype(jnp.float32)
    far_place = leafs + core_f * leafs + chip_f * EXPORT + jnp.minimum(rank8, EXPORT - 1.0)
    relative = (lane8 - my_start).astype(jnp.float32)
    place = jnp.where(lane8 >= my_start, relative, far_place)

    slot_row = lax.broadcasted_iota(jnp.int32, (32, node_total), 0)
    slot_col = lax.broadcasted_iota(jnp.int32, (32, node_total), 1)
    own_here = slot_col == my_start + slot_row
    own_mask = jnp.dot(
        jnp.where(own_here, 1.0, 0.0).astype(jnp.bfloat16),
        jnp.where(mask > 0, 1.0, 0.0).astype(jnp.bfloat16),
        preferred_element_type=jnp.float32,
    )
    others = jnp.where((own_mask > 0.5) & ~own_here, 1.0, 0.0)
    before = jnp.where(row_id < col_id, 1.0, 0.0).astype(jnp.bfloat16)
    rank = jnp.dot(others.astype(jnp.bfloat16), before, preferred_element_type=jnp.float32)
    lane32 = lax.broadcasted_iota(jnp.int32, (32, 128), 1)
    row32 = lax.broadcasted_iota(jnp.int32, (32, 128), 0)
    table = jnp.zeros((32, 128), jnp.float32)
    for r in range(ANC - 1):
        hit = (others > 0.5) & (jnp.abs(rank - float(r)) < 0.5)
        value = jnp.sum(jnp.where(hit, place[0:1, :], 0.0), axis=1, keepdims=True)
        table = jnp.where(lane32 == r, value, table)
    table = jnp.where(lane32 == ANC - 1, jnp.sum(others, axis=1, keepdims=True), table)

    pltpu.make_async_copy(ids_in.at[pl.ds(0, leafs - 1)], ids_in.at[pl.ds(0, leafs - 1)], ids_recv).wait()

    def sources(s, total):
        return total + jnp.where(ids_in[s][0:1, :] == my_start + row32, s.astype(jnp.float32), 0.0)

    source = lax.fori_loop(0, leafs, sources, jnp.zeros((32, 128), jnp.float32))
    table = jnp.where(lane32 == 2 * ANC, source, table)
    table_ref[...] = table.astype(jnp.int32)
    mine8 = (lane8 >= my_start) & (owner == me) & (seen8 > 0.5)
    for k in range(EXPORT):
        picked = jnp.sum(
            jnp.where(mine8 & (jnp.abs(rank8 - float(k)) < 0.5), relative, 0.0), axis=1, keepdims=True
        )
        chosen = jnp.sum(
            jnp.where(row32.astype(jnp.float32) == picked[0:1, :], source, 0.0), axis=0, keepdims=True
        )
        export_src[k] = jnp.broadcast_to(chosen, (TOK, 128))

    for load in loads:
        load.wait()
    full_arrival(0, 0).wait_recv()
    forward(0, 0).start()
    full_arrival(1, 0).wait_recv()
    forward(1, 0).start()
    full(0, 2).start()
    full(1, 2).start()

    def accumulate(src, c, first):
        wide = pieces[src, c].reshape(rows, feat).astype(jnp.float32)
        gain = gain_ref[src]
        scaled[...] = (wide * gain).astype(jnp.bfloat16)
        part = jnp.sum(wide * wide, axis=1, keepdims=True)
        if first:
            squares[...] = jnp.broadcast_to(part, (rows, 128))
        else:
            squares[...] += jnp.broadcast_to(part, (rows, 128))
        product = jnp.dot(scaled[...], weights[src], preferred_element_type=jnp.float32)
        if first:
            acc[...] = product
        else:
            acc[...] += product

    def slot_copy(o, c):
        peer = lax.rem(me + o, leafs)
        return pltpu.make_async_remote_copy(
            src_ref=send.at[c, peer],
            dst_ref=recv.at[c, me],
            send_sem=slot_send.at[c],
            recv_sem=slot_recv.at[c],
            device_id=(peer, z),
            device_id_type=MESH,
        )

    def slots_arrived(c):
        part = recv.at[c, pl.ds(0, leafs - 1)]
        pltpu.make_async_copy(part, part, slot_recv.at[c]).wait()

    def qkv_out(c):
        return pltpu.make_async_copy(
            recv.at[c], qkv_ref.at[:, pl.ds(pl.multiple_of(c * TOK, TOK), TOK), :], qkv_sem.at[c]
        )

    def far_out(c):
        return pltpu.make_async_copy(
            far.at[c], far_ref.at[:, pl.ds(pl.multiple_of(c * TOK, TOK), TOK), :], far_sem.at[c]
        )

    block = ((core * 4 + cy) * 4 + cx) * EXPORT

    def x_copy(o, c):
        part = far.at[c, pl.ds(block, EXPORT)]
        peer = (cy * 4 + lax.rem(cx + o, 4)) * 2 + core
        return pltpu.make_async_remote_copy(
            src_ref=part, dst_ref=part, send_sem=x_send.at[o - 1, c], recv_sem=x_recv.at[o - 1, c],
            device_id=(peer, z), device_id_type=MESH,
        )

    def x_arrival(o, c):
        part = far.at[c, pl.ds(((core * 4 + cy) * 4 + lax.rem(cx + 4 - o, 4)) * EXPORT, EXPORT)]
        return pltpu.make_async_remote_copy(
            src_ref=part, dst_ref=part, send_sem=x_send.at[o - 1, c], recv_sem=x_recv.at[o - 1, c],
            device_id=(me, right), device_id_type=MESH,
        )

    def y_copy(o, c):
        part = far.at[c, pl.ds((core * 4 + cy) * 4 * EXPORT, 4 * EXPORT)]
        peer = (lax.rem(cy + o, 4) * 4 + cx) * 2 + core
        return pltpu.make_async_remote_copy(
            src_ref=part, dst_ref=part, send_sem=y_send.at[o - 1, c], recv_sem=y_recv.at[o - 1, c],
            device_id=(peer, z), device_id_type=MESH,
        )

    def y_arrival(o, c):
        part = far.at[c, pl.ds((core * 4 + lax.rem(cy + 4 - o, 4)) * 4 * EXPORT, 4 * EXPORT)]
        return pltpu.make_async_remote_copy(
            src_ref=part, dst_ref=part, send_sem=y_send.at[o - 1, c], recv_sem=y_recv.at[o - 1, c],
            device_id=(me, right), device_id_type=MESH,
        )

    def core_copy(c):
        part = far.at[c, pl.ds(core * 16 * EXPORT, 16 * EXPORT)]
        return pltpu.make_async_remote_copy(
            src_ref=part, dst_ref=part, send_sem=core_send.at[c], recv_sem=core_recv.at[c],
            device_id=(chip * 2 + 1 - core, z), device_id_type=MESH,
        )

    def core_arrival(c):
        part = far.at[c, pl.ds((1 - core) * 16 * EXPORT, 16 * EXPORT)]
        return pltpu.make_async_remote_copy(
            src_ref=part, dst_ref=part, send_sem=core_send.at[c], recv_sem=core_recv.at[c],
            device_id=(chip * 2 + 1 - core, z), device_id_type=MESH,
        )

    def export_x(c):
        slots_arrived(c)
        qkv_out(c).start()
        for k in range(EXPORT):
            for t in range(2 * k_cols // 128):
                lanes = pl.ds(q_cols + t * 128, 128)

                def pick(s, total):
                    return jnp.where(
                        export_src[k] == s.astype(jnp.float32), recv[c, s, :, lanes].astype(jnp.float32), total
                    )

                chosen = lax.fori_loop(0, leafs, pick, jnp.zeros((TOK, 128), jnp.float32))
                far[c, block + k, :, pl.ds(t * 128, 128)] = chosen.astype(jnp.bfloat16)
        for o in (1, 2, 3):
            x_copy(o, c).start()

    def export_y(c):
        for o in (1, 2, 3):
            x_arrival(o, c).wait_recv()
        for o in (1, 2, 3):
            y_copy(o, c).start()

    def export_core(c):
        for o in (1, 2, 3):
            y_arrival(o, c).wait_recv()
        core_copy(c).start()

    def one_chunk(c, carry):
        accumulate(z, c, True)
        accumulate(left, c, False)
        accumulate(right, c, False)

        @pl.when(c + 1 < CHUNKS)
        def _():
            full_arrival(0, c + 1).wait_recv()
            forward(0, c + 1).start()
            full_arrival(1, c + 1).wait_recv()
            forward(1, c + 1).start()

        @pl.when(c + 3 < CHUNKS)
        def _():
            full(0, c + 3).start()
            full(1, c + 3).start()

        @pl.when(c >= 2)
        def _():
            export_y(c - 2)

        forward_arrival(0, c).wait_recv()
        forward_arrival(1, c).wait_recv()
        accumulate(opposite, c, False)

        scale = lax.rsqrt(squares[...] / width + norm_epsilon)
        cosine = angle_cos[c]
        sine = angle_sin[c]
        for head in range(cols // HD):
            at = pl.ds(head * HD, HD)
            value = acc[:, at] * scale
            if head * HD < q_cols + k_cols:
                value = value * cosine + pltpu.roll(value, HD // 2, 1) * sine
            made[:, :, at] = value.astype(jnp.bfloat16).reshape(nodes, TOK, HD)

        def fill(d, carry2):
            send[c, d] = made[index_sm[d]]
            return carry2

        lax.fori_loop(0, leafs, fill, 0)
        lax.fori_loop(1, leafs, lambda o, carry2: (slot_copy(o, c).start(), carry2)[1], 0)
        recv[c, me] = send[c, me]

        @pl.when(c >= 2)
        def _():
            export_core(c - 2)

        @pl.when(c >= 1)
        def _():
            export_x(c - 1)

        return carry

    lax.fori_loop(0, CHUNKS, one_chunk, 0)

    last = CHUNKS - 1
    export_y(last - 1)
    export_x(last)
    export_core(last - 1)
    export_y(last)
    export_core(last)

    def settle(c, carry):
        core_arrival(c).wait_recv()
        far_out(c).start()
        for side in (0, 1):
            full(side, c).wait_send()
            forward(side, c).wait_send()
        sent = send.at[c, pl.ds(0, leafs - 1)]
        pltpu.make_async_copy(sent, sent, slot_send.at[c]).wait()
        for o in (1, 2, 3):
            x_copy(o, c).wait_send()
            y_copy(o, c).wait_send()
        core_copy(c).wait_send()
        qkv_out(c).wait()
        far_out(c).wait()
        return carry

    lax.fori_loop(0, CHUNKS, settle, 0)
    pltpu.make_async_copy(ids_out.at[pl.ds(0, leafs - 1)], ids_out.at[pl.ds(0, leafs - 1)], ids_send).wait()


def project(tokens, gain, freq, w_query, w_key, w_value, gen_node, partition, parent, block_mask, leafs):
    nodes = gen_node.shape[0]
    feat = tokens.shape[1]
    width = gain.shape[-1] * 4
    q_cols = w_query.shape[1]
    k_cols = w_key.shape[1]
    cols = q_cols + 2 * k_cols
    rows = nodes * TOK
    node_total = parent.shape[0]
    bf16, f32, i32 = jnp.bfloat16, jnp.float32, jnp.int32
    dma = pltpu.SemaphoreType.DMA
    smem = pl.BlockSpec(memory_space=pltpu.SMEM)
    vmem = pl.BlockSpec(memory_space=pltpu.VMEM)
    hbm = pl.BlockSpec(memory_space=pl.ANY)
    return pl.pallas_call(
        functools.partial(project_kernel, leafs, nodes, width, q_cols, k_cols),
        out_shape=(
            jax.ShapeDtypeStruct((leafs, NODE_TOK, cols), bf16),
            jax.ShapeDtypeStruct((leafs * EXPORT, NODE_TOK, 2 * k_cols), bf16),
            jax.ShapeDtypeStruct((32, 128), i32),
        ),
        in_specs=[smem, smem, smem, vmem, vmem, vmem, hbm, hbm, hbm, hbm],
        out_specs=(hbm, hbm, vmem),
        scratch_shapes=[
            pltpu.VMEM((4, CHUNKS, nodes, TOK, feat), bf16),
            pltpu.VMEM((4, feat, cols), bf16),
            pltpu.VMEM((rows, feat), bf16),
            pltpu.VMEM((rows, cols), f32),
            pltpu.VMEM((rows, 128), f32),
            pltpu.VMEM((CHUNKS, rows, HD), f32),
            pltpu.VMEM((CHUNKS, rows, HD), f32),
            pltpu.VMEM((nodes, TOK, cols), bf16),
            pltpu.VMEM((CHUNKS, leafs, TOK, cols), bf16),
            pltpu.VMEM((CHUNKS, leafs, TOK, cols), bf16),
            pltpu.VMEM((CHUNKS, leafs * EXPORT, TOK, 2 * k_cols), bf16),
            pltpu.VMEM((leafs, 8, 128), i32),
            pltpu.VMEM((leafs, 8, 128), i32),
            pltpu.VMEM((EXPORT, TOK, 128), f32),
            pltpu.SMEM((node_total,), i32),
            pltpu.SMEM((leafs,), i32),
            pltpu.SMEM((leafs,), i32),
            pltpu.SMEM((leafs,), i32),
            dma((3,)),
            dma((CHUNKS,)),
            dma((2, CHUNKS)),
            dma((2, CHUNKS)),
            dma((2, CHUNKS)),
            dma((2, CHUNKS)),
            dma,
            dma,
            dma((CHUNKS,)),
            dma((CHUNKS,)),
            dma((CHUNKS,)),
            dma((CHUNKS,)),
            dma((CHUNKS,)),
            dma((3, CHUNKS)),
            dma((3, CHUNKS)),
            dma((3, CHUNKS)),
            dma((3, CHUNKS)),
            dma((CHUNKS,)),
            dma((CHUNKS,)),
        ],
        compiler_params=pltpu.CompilerParams(
            collective_id=0, has_side_effects=True, vmem_limit_bytes=60 * 1024 * 1024
        ),
        cost_estimate=pl.CostEstimate(
            flops=2 * nodes * NODE_TOK * width * cols, bytes_accessed=30_000_000, transcendentals=0
        ),
        name="project_exchange",
    )(
        gen_node, partition, parent, block_mask, gain, freq,
        tokens.reshape(nodes, NODE_TOK, feat),
        w_query.reshape(4, feat, q_cols), w_key.reshape(4, feat, k_cols), w_value.reshape(4, feat, k_cols),
    )


def attend_kernel(
    q_cols, k_cols, table_ref, count_ref, qkv_ref, far_ref, out_ref, query, pool, load_sem
):
    leafs = qkv_ref.shape[0]
    loads = [
        pltpu.make_async_copy(qkv_ref.at[:, :, pl.ds(0, q_cols)], query, load_sem.at[0]),
        pltpu.make_async_copy(
            qkv_ref.at[:, :, pl.ds(q_cols, 2 * k_cols)], pool.at[pl.ds(0, leafs)], load_sem.at[1]
        ),
        pltpu.make_async_copy(far_ref, pool.at[pl.ds(leafs, far_ref.shape[0])], load_sem.at[2]),
    ]
    for load in loads:
        load.start()
    out_ref[...] = jnp.zeros_like(out_ref)
    for load in loads:
        load.wait()
    count = count_ref[0]
    heads = k_cols // HD
    groups = q_cols // k_cols
    q_rows = groups * NODE_TOK

    def attend(r, blocks, seen):
        own = table_ref[r, 2 * ANC]
        places = [own]
        for p in range(1, blocks):
            v = table_ref[r, p - 1]
            near = table_ref[jnp.minimum(v, leafs - 1), 2 * ANC]
            place = jnp.where(v < leafs, near, v)
            places.append(jnp.where(p < seen, place, own))
        width = blocks * NODE_TOK
        key_col = lax.broadcasted_iota(jnp.int32, (q_rows, width), 1)
        query_tok = lax.rem(lax.broadcasted_iota(jnp.int32, (q_rows, width), 0), NODE_TOK)
        allowed = ((key_col >= NODE_TOK) | (key_col <= query_tok)) & (key_col < seen * NODE_TOK)
        at = pl.ds(pl.multiple_of(r * NODE_TOK, NODE_TOK), NODE_TOK)
        for h in range(heads):
            keys = jnp.concatenate([pool[p, :, pl.ds(h * HD, HD)] for p in places], axis=0)
            values = jnp.concatenate([pool[p, :, pl.ds(k_cols + h * HD, HD)] for p in places], axis=0)
            queries = jnp.concatenate(
                [query[own, :, pl.ds((h * groups + g) * HD, HD)] for g in range(groups)], axis=0
            )
            scores = lax.dot_general(
                queries, keys, (((1,), (1,)), ((), ())), preferred_element_type=jnp.float32
            )
            capped = jnp.tanh(scores * (query_scale / soft_cap)) * soft_cap
            probs = jnp.where(allowed, jnp.exp(capped), 0.0)
            totals = jnp.sum(probs, axis=1, keepdims=True)
            numer = jnp.dot(probs.astype(jnp.bfloat16), values, preferred_element_type=jnp.float32)
            result = (numer / totals).astype(jnp.bfloat16)
            for g in range(groups):
                out_ref[at, pl.ds((h * groups + g) * HD, HD)] = result[g * NODE_TOK : (g + 1) * NODE_TOK]

    def one_node(r, carry):
        seen = table_ref[r, ANC - 1] + 1
        for low, high in ((0, 2), (2, 4), (4, 6), (6, 8)):

            @pl.when((seen > low) & (seen <= high))
            def _(high=high):
                attend(r, high, seen)

        return carry

    lax.fori_loop(0, count, one_node, 0)


def attend_all(table, count, qkv, far, q_cols, k_cols):
    bf16 = jnp.bfloat16
    leafs = qkv.shape[0]
    hbm = pl.BlockSpec(memory_space=pl.ANY)
    return pl.pallas_call(
        functools.partial(attend_kernel, q_cols, k_cols),
        out_shape=jax.ShapeDtypeStruct((CAP * NODE_TOK, q_cols), bf16),
        grid_spec=pltpu.PrefetchScalarGridSpec(
            num_scalar_prefetch=2,
            grid=(),
            in_specs=[hbm, hbm],
            out_specs=pl.BlockSpec(memory_space=pltpu.VMEM),
            scratch_shapes=[
                pltpu.VMEM((leafs, NODE_TOK, q_cols), bf16),
                pltpu.VMEM((leafs + far.shape[0], NODE_TOK, 2 * k_cols), bf16),
                pltpu.SemaphoreType.DMA((3,)),
            ],
        ),
        compiler_params=pltpu.CompilerParams(vmem_limit_bytes=40 * 1024 * 1024),
        name="attend",
    )(table, count, qkv, far)


def on_device(tokens, norm_gain, w_query, w_key, w_value, gen_node, partition, parent, block_mask):
    leafs = lax.axis_size("leaf")
    leaf_index = lax.axis_index("leaf")
    feat = tokens.shape[1]
    gain = norm_gain.astype(jnp.float32).reshape(-1, 1, feat)
    half_dim = HD // 2
    inverse_freq = jnp.exp(jnp.arange(half_dim, dtype=jnp.float32) * (-2.0 * math.log(rope_base) / HD))
    freq = jnp.concatenate([inverse_freq, inverse_freq])[None, :]
    qkv, far, table = project(
        tokens, gain, freq, w_query, w_key, w_value, gen_node, partition, parent, block_mask, leafs
    )
    count = lax.dynamic_slice(partition, (leaf_index,), (1,))
    return attend_all(table, count, qkv, far, w_query.shape[1], w_key.shape[1])


def solution(mesh):
    in_specs = (
        P("leaf", "mp"),
        P(),
        P(None, "mp"),
        P(None, "mp"),
        P(None, "mp"),
        P("leaf"),
        P(),
        P(),
        P(),
    )
    out_specs = P("leaf", "mp")
    return jax.shard_map(
        on_device, mesh=mesh, in_specs=in_specs, out_specs=out_specs, check_vma=False
    )
```

```python
import functools
import math

import jax
import jax.numpy as jnp
import numpy as np
from jax import lax
from jax.experimental import pallas as pl
from jax.experimental.pallas import tpu as pltpu
from jax.sharding import PartitionSpec as P

HD = 128
CAP = 31
ANC = 8
EXPORT = 2
CHUNKS = 4
NODE_TOK = 64
TOK = NODE_TOK // CHUNKS
SLOTS = CAP
BATCH = 4

norm_epsilon = 1e-06
soft_cap = 50.0
query_scale = 144.0 ** (-0.5)
rope_base = 10000.0

MESH = pl.DeviceIdType.MESH


def fused_kernel(
    leafs, nodes, width, q_cols, k_cols,
    gen_ref, part_ref, parent_ref, mask_ref, gain_ref, freq_ref, tok_ref, wq_ref, wk_ref, wv_ref,
    out_ref,
    pieces, weights, scaled, acc, squares, angle_cos, angle_sin, made, send, recv, far,
    query, pool, numer, total, ids_out, ids_in, table_vm, gain_vm,
    depth_sm, index_sm, start_sm, end_sm, table_sm, place_sm,
    load_sem, own_sem, full_send, full_recv, half_send, half_recv, ids_send, ids_recv, table_sem,
    slot_send, slot_recv, chip_send, chip_recv, core_send, core_recv,
):
    me = lax.axis_index("leaf")
    z = lax.axis_index("mp")
    mp = 4
    right, left = lax.rem(z + 1, mp), lax.rem(z + 3, mp)
    opposite = lax.rem(z + 2, mp)
    feat = width // mp
    rows = nodes * TOK
    cols = q_cols + 2 * k_cols
    half = nodes // 2
    node_total = parent_ref.shape[0]
    core = lax.rem(me, 2)
    chip = lax.div(me, 2)
    chips = leafs // 2

    loads = [
        pltpu.make_async_copy(wq_ref, weights.at[:, :, pl.ds(0, q_cols)], load_sem.at[0]),
        pltpu.make_async_copy(wk_ref, weights.at[:, :, pl.ds(q_cols, k_cols)], load_sem.at[1]),
        pltpu.make_async_copy(wv_ref, weights.at[:, :, pl.ds(q_cols + k_cols, k_cols)], load_sem.at[2]),
    ]

    def own_load(c):
        return pltpu.make_async_copy(
            tok_ref.at[:, pl.ds(pl.multiple_of(c * TOK, TOK), TOK), :], pieces.at[z, c], own_sem.at[c]
        )

    barrier = pltpu.get_barrier_semaphore()

    def greet(o, carry):
        peer = lax.rem(me + o, leafs)
        pl.semaphore_signal(barrier, inc=1, device_id=(peer, z), device_id_type=MESH)
        return carry

    lax.fori_loop(1, leafs, greet, 0)
    pl.semaphore_signal(barrier, inc=1, device_id=(me, right), device_id_type=MESH)
    pl.semaphore_signal(barrier, inc=1, device_id=(me, left), device_id_type=MESH)
    for c in range(CHUNKS):
        own_load(c).start()
    for load in loads:
        load.start()
    pl.semaphore_wait(barrier, leafs + 1)

    def full(side, part, c):
        piece = pieces.at[z, c, pl.ds(part * half, half)]
        return pltpu.make_async_remote_copy(
            src_ref=piece,
            dst_ref=piece,
            send_sem=full_send.at[side, part, c],
            recv_sem=full_recv.at[side, part, c],
            device_id=(me, right if side == 0 else left),
            device_id_type=MESH,
        )

    def full_arrival(side, part, c):
        piece = pieces.at[left if side == 0 else right, c, pl.ds(part * half, half)]
        return pltpu.make_async_remote_copy(
            src_ref=piece,
            dst_ref=piece,
            send_sem=full_send.at[side, part, c],
            recv_sem=full_recv.at[side, part, c],
            device_id=(me, right if side == 0 else left),
            device_id_type=MESH,
        )

    def forward(side, c):
        source = left if side == 0 else right
        part = pieces.at[source, c, pl.ds(side * half, half)]
        return pltpu.make_async_remote_copy(
            src_ref=part,
            dst_ref=part,
            send_sem=half_send.at[side, c],
            recv_sem=half_recv.at[side, c],
            device_id=(me, right if side == 0 else left),
            device_id_type=MESH,
        )

    def forward_arrival(side, c):
        part = pieces.at[opposite, c, pl.ds(side * half, half)]
        return pltpu.make_async_remote_copy(
            src_ref=part,
            dst_ref=part,
            send_sem=half_send.at[side, c],
            recv_sem=half_recv.at[side, c],
            device_id=(me, right if side == 0 else left),
            device_id_type=MESH,
        )

    for c in range(CHUNKS):
        own_load(c).wait()
        if c == 0:
            for step in (0, 1):
                for side in (0, 1):
                    full(side, side ^ step, 0).start()

    def pass_on(c):
        for side in (0, 1):
            full_arrival(side, side, c).wait_recv()
            forward(side, c).start()

        @pl.when(c + 1 < CHUNKS)
        def _():
            for side in (0, 1):
                full(side, side, c + 1).start()

        for side in (0, 1):
            full_arrival(side, 1 - side, c).wait_recv()

        @pl.when(c + 1 < CHUNKS)
        def _():
            for side in (0, 1):
                full(side, 1 - side, c + 1).start()

    for part in range(mp):
        gain_vm[part] = gain_ref[pl.ds(part * feat, feat)].astype(jnp.float32).reshape(1, feat)

    def ranges(d, first):
        last = first + part_ref[d]
        start_sm[d] = first
        end_sm[d] = last
        found = jnp.int32(0)
        for b in range(nodes):
            node = gen_ref[b]
            found = found + jnp.where((node >= first) & (node < last), b + 1, 0)
        local = jnp.clip(found - 1, 0, nodes - 1)
        index_sm[d] = local
        ids_out[d] = jnp.full((8, 128), jnp.where(found > 0, gen_ref[local], -1), jnp.int32)
        return last

    lax.fori_loop(0, leafs, ranges, jnp.int32(0))

    def ids_copy(o):
        peer = lax.rem(me + o, leafs)
        return pltpu.make_async_remote_copy(
            src_ref=ids_out.at[peer],
            dst_ref=ids_in.at[me],
            send_sem=ids_send,
            recv_sem=ids_recv,
            device_id=(peer, z),
            device_id_type=MESH,
        )

    lax.fori_loop(1, leafs, lambda o, carry: (ids_copy(o).start(), carry)[1], 0)
    ids_in[me] = ids_out[me]

    depth_sm[0] = jnp.int32(0)

    def deeper(n, carry):
        depth_sm[n] = depth_sm[parent_ref[n]] + 1
        return carry

    lax.fori_loop(1, node_total, deeper, 0)

    pass_on(jnp.int32(0))

    token_row = lax.broadcasted_iota(jnp.int32, (TOK, HD), 0)
    sign = jnp.where(lax.broadcasted_iota(jnp.int32, (rows, HD), 1) < HD // 2, -1.0, 1.0)

    def tables(c, carry):
        def one_node(b, carry2):
            position = depth_sm[gen_ref[b]] * NODE_TOK + c * TOK + token_row
            at = pl.ds(pl.multiple_of(b * TOK, TOK), TOK)
            angle_cos[c, at, :] = position.astype(jnp.float32) * freq_ref[...]
            return carry2

        lax.fori_loop(0, nodes, one_node, 0)
        angles = angle_cos[c]
        angle_sin[c] = jnp.sin(angles) * sign
        angle_cos[c] = jnp.cos(angles)
        return carry

    lax.fori_loop(0, CHUNKS, tables, 0)

    lane8 = lax.broadcasted_iota(jnp.int32, (8, node_total), 1)

    def spans(step, carry):
        d = leafs - 1 - step
        end_of, start_of, owner = carry
        inside = lane8 < end_sm[d]
        return (
            jnp.where(inside, end_sm[d], end_of),
            jnp.where(inside, start_sm[d], start_of),
            jnp.where(inside, d, owner),
        )

    blank = jnp.zeros((8, node_total), jnp.int32)
    end_of, start_of, owner = lax.fori_loop(0, leafs, spans, (blank, blank, blank))
    my_start = start_sm[me]
    row_id = lax.broadcasted_iota(jnp.int32, (node_total, node_total), 0)
    col_id = lax.broadcasted_iota(jnp.int32, (node_total, node_total), 1)
    mask = mask_ref[...]
    foreign = (mask > 0) & (row_id >= end_of[0:1, :])
    seen = jnp.max(jnp.where(foreign, 1.0, 0.0), axis=0, keepdims=True)
    earlier = jnp.where((row_id < col_id) & (row_id >= start_of[0:1, :]), 1.0, 0.0).astype(jnp.bfloat16)
    seen8 = jnp.broadcast_to(seen, (8, node_total))
    rank8 = jnp.dot(seen8.astype(jnp.bfloat16), earlier, preferred_element_type=jnp.float32)
    owner_f = owner.astype(jnp.float32)
    core_f = lax.rem(owner, 2).astype(jnp.float32)
    chip_f = lax.div(owner, 2).astype(jnp.float32)
    far_place = leafs + core_f * leafs + chip_f * EXPORT + jnp.minimum(rank8, EXPORT - 1.0)
    relative = (lane8 - my_start).astype(jnp.float32)
    place = jnp.where(lane8 >= my_start, relative, far_place)

    slot_row = lax.broadcasted_iota(jnp.int32, (32, node_total), 0)
    slot_col = lax.broadcasted_iota(jnp.int32, (32, node_total), 1)
    own_here = slot_col == my_start + slot_row
    own_mask = jnp.dot(
        jnp.where(own_here, 1.0, 0.0).astype(jnp.bfloat16),
        jnp.where(mask > 0, 1.0, 0.0).astype(jnp.bfloat16),
        preferred_element_type=jnp.float32,
    )
    others = jnp.where((own_mask > 0.5) & ~own_here, 1.0, 0.0)
    before = jnp.where(row_id < col_id, 1.0, 0.0).astype(jnp.bfloat16)
    rank = jnp.dot(others.astype(jnp.bfloat16), before, preferred_element_type=jnp.float32)
    lane32 = lax.broadcasted_iota(jnp.int32, (32, 128), 1)
    row32 = lax.broadcasted_iota(jnp.int32, (32, 128), 0)
    table = jnp.zeros((32, 128), jnp.float32)
    for r in range(ANC - 1):
        hit = (others > 0.5) & (jnp.abs(rank - float(r)) < 0.5)
        value = jnp.sum(jnp.where(hit, place[0:1, :], 0.0), axis=1, keepdims=True)
        table = jnp.where(lane32 == r, value, table)
    table = jnp.where(lane32 == ANC - 1, jnp.sum(others, axis=1, keepdims=True), table)

    pltpu.make_async_copy(ids_in.at[pl.ds(0, leafs - 1)], ids_in.at[pl.ds(0, leafs - 1)], ids_recv).wait()

    def sources(s, total):
        return total + jnp.where(ids_in[s][0:1, :] == my_start + row32, s.astype(jnp.float32), 0.0)

    source = lax.fori_loop(0, leafs, sources, jnp.zeros((32, 128), jnp.float32))
    table = jnp.where(lane32 == 2 * ANC, source, table)
    mine8 = (lane8 >= my_start) & (owner == me) & (seen8 > 0.5)
    for k in range(EXPORT):
        picked = jnp.sum(
            jnp.where(mine8 & (jnp.abs(rank8 - float(k)) < 0.5), relative, 0.0), axis=1, keepdims=True
        )
        chosen = jnp.sum(
            jnp.where(row32.astype(jnp.float32) == picked[0:1, :], source, 0.0), axis=0, keepdims=True
        )
        table = jnp.where(lane32 == 2 * ANC + 1 + k, chosen, table)
    table_vm[...] = table.astype(jnp.int32)
    to_scalars = pltpu.make_async_copy(table_vm, table_sm, table_sem)
    to_scalars.start()
    to_scalars.wait()

    def find_places(r, carry):
        place_sm[r * ANC] = jnp.clip(table_sm[r, 2 * ANC], 0, leafs - 1)
        for p in range(ANC - 1):
            v = table_sm[r, p]
            near = table_sm[jnp.clip(v, 0, leafs - 1), 2 * ANC]
            place_sm[r * ANC + p + 1] = jnp.clip(jnp.where(v < leafs, near, v), 0, leafs + leafs * EXPORT - 1)
        return carry

    lax.fori_loop(0, SLOTS, find_places, 0)
    my_count = part_ref[me]

    for load in loads:
        load.wait()
    def accumulate(src, c, first):
        wide = pieces[src, c].reshape(rows, feat).astype(jnp.float32)
        gain = gain_vm[src]
        scaled[...] = (wide * gain).astype(jnp.bfloat16)
        part = jnp.sum(wide * wide, axis=1, keepdims=True)
        if first:
            squares[...] = jnp.broadcast_to(part, (rows, 128))
        else:
            squares[...] += jnp.broadcast_to(part, (rows, 128))
        product = jnp.dot(scaled[...], weights[src], preferred_element_type=jnp.float32)
        if first:
            acc[...] = product
        else:
            acc[...] += product

    def slot_copy(o, c):
        peer = lax.rem(me + o, leafs)
        return pltpu.make_async_remote_copy(
            src_ref=send.at[c, peer],
            dst_ref=recv.at[c, me],
            send_sem=slot_send.at[c],
            recv_sem=slot_recv.at[c],
            device_id=(peer, z),
            device_id_type=MESH,
        )

    def slots_arrived(c):
        part = recv.at[c, pl.ds(0, leafs - 1)]
        pltpu.make_async_copy(part, part, slot_recv.at[c]).wait()

    block = core * chips * EXPORT + chip * EXPORT

    def chip_copy(o, c):
        part = far.at[c, pl.ds(block, EXPORT)]
        return pltpu.make_async_remote_copy(
            src_ref=part, dst_ref=part, send_sem=chip_send.at[c], recv_sem=chip_recv.at[c],
            device_id=(lax.rem(chip + o, chips) * 2 + core, z), device_id_type=MESH,
        )

    def chips_arrived(c):
        part = far.at[c, pl.ds(0, (chips - 1) * EXPORT)]
        pltpu.make_async_copy(part, part, chip_recv.at[c]).wait()

    def core_copy(c):
        part = far.at[c, pl.ds(core * chips * EXPORT, chips * EXPORT)]
        return pltpu.make_async_remote_copy(
            src_ref=part, dst_ref=part, send_sem=core_send.at[c], recv_sem=core_recv.at[c],
            device_id=(chip * 2 + 1 - core, z), device_id_type=MESH,
        )

    def core_arrival(c):
        part = far.at[c, pl.ds((1 - core) * chips * EXPORT, chips * EXPORT)]
        return pltpu.make_async_remote_copy(
            src_ref=part, dst_ref=part, send_sem=core_send.at[c], recv_sem=core_recv.at[c],
            device_id=(chip * 2 + 1 - core, z), device_id_type=MESH,
        )

    kv_cols = 2 * k_cols

    def export_start(c):
        slots_arrived(c)

        def keep(s, carry):
            query[c, s] = recv[c, s, :, pl.ds(0, q_cols)]
            pool[c, s] = recv[c, s, :, pl.ds(q_cols, kv_cols)]
            return carry

        lax.fori_loop(0, leafs, keep, 0)
        for k in range(EXPORT):
            far[c, block + k] = pool[c, jnp.clip(table_sm[0, 2 * ANC + 1 + k], 0, leafs - 1)]
        lax.fori_loop(1, chips, lambda o, carry: (chip_copy(o, c).start(), carry)[1], 0)

    def export_core(c):
        chips_arrived(c)
        core_copy(c).start()

    def export_end(c):
        core_arrival(c).wait_recv()

        def keep(s, carry):
            pool[c, leafs + s] = far[c, s]
            return carry

        lax.fori_loop(0, leafs * EXPORT, keep, 0)

    heads = k_cols // HD
    groups = q_cols // k_cols
    q_rows = groups * TOK
    lane = lax.broadcasted_iota(jnp.int32, (1, ANC * TOK), 1)

    tri = lax.broadcasted_iota(jnp.int32, (q_rows, ANC * TOK), 1) <= lax.rem(
        lax.broadcasted_iota(jnp.int32, (q_rows, ANC * TOK), 0), TOK
    )
    tri = tri | (lax.broadcasted_iota(jnp.int32, (q_rows, ANC * TOK), 1) >= TOK)

    def load_queries(own, h, first, last):
        return jnp.concatenate(
            [
                query[c, own, :, pl.ds((h * groups + g) * HD, HD)]
                for c in range(first, last)
                for g in range(groups)
            ],
            axis=0,
        )

    def load_pool(places, column, first, last):
        return jnp.concatenate(
            [pool[c, p, :, pl.ds(column, HD)] for c in range(first, last) for p in places], axis=0
        )

    def attend(q0, q1, k0, k1, final):
        at = pl.ds(q0 * q_rows, (q1 - q0) * q_rows)

        def batch(slots):
            chains = [(n, h) for n in range(len(slots)) for h in range(heads)]
            places = [[place_sm[r * ANC + p] for p in range(ANC)] for r in slots]
            limit = [lane < (table_sm[r, ANC - 1] + 1) * TOK for r in slots]
            past = [x & (lane >= TOK) for x in limit]
            scores = {
                (n, h): lax.dot_general(
                    load_queries(places[n][0], h, q0, q1),
                    load_pool(places[n], h * HD, k0, k1),
                    (((1,), (1,)), ((), ())),
                    preferred_element_type=jnp.float32,
                )
                for n, h in chains
            }
            probs, sums = {}, {}
            for n, h in chains:
                capped = jnp.tanh(scores[n, h] * (query_scale / soft_cap))
                raised = jnp.exp2(capped * (soft_cap * math.log2(math.e)))
                lines, adds = [], []
                for q in range(q0, q1):
                    tiles = []
                    for k in range(k0, k1):
                        tile = raised[
                            (q - q0) * q_rows : (q - q0 + 1) * q_rows,
                            (k - k0) * ANC * TOK : (k - k0 + 1) * ANC * TOK,
                        ]
                        keep = limit[n] if k < q else past[n] if k > q else limit[n] & tri
                        tiles.append(jnp.where(keep, tile, 0.0))
                    lines.append(jnp.concatenate(tiles, axis=1))
                    adds.append(functools.reduce(lambda x, y: x + y, tiles))
                probs[n, h] = jnp.concatenate(lines, axis=0).astype(jnp.bfloat16)
                sums[n, h] = jnp.concatenate(adds, axis=0)
            parts = {
                (n, h): jnp.dot(
                    probs[n, h],
                    load_pool(places[n], k_cols + h * HD, k0, k1),
                    preferred_element_type=jnp.float32,
                )
                for n, h in chains
            }
            if not final:
                for n, h in chains:
                    numer[slots[n], h, at, :] = parts[n, h]
                    total[slots[n], h, at, :] = sums[n, h]
                return
            results = {}
            for n, h in chains:
                whole = jnp.sum(total[slots[n], h] + sums[n, h], axis=1, keepdims=True)
                result = (numer[slots[n], h] + parts[n, h]) * (1.0 / whole)
                results[n, h] = jnp.where(slots[n] < my_count, result, 0.0).astype(jnp.bfloat16)
            for n, h in chains:
                for q in range(CHUNKS):
                    for g in range(groups):
                        start = (q * groups + g) * TOK
                        out_ref[slots[n], pl.ds(q * TOK, TOK), pl.ds((h * groups + g) * HD, HD)] = results[n, h][
                            start : start + TOK
                        ]

        def step(i, carry):
            batch([i * BATCH + n for n in range(BATCH)])
            return carry

        lax.fori_loop(0, SLOTS // BATCH, step, 0)
        if SLOTS % BATCH:
            batch(list(range(SLOTS // BATCH * BATCH, SLOTS)))

    def one_chunk(c, carry):
        accumulate(z, c, True)
        accumulate(left, c, False)
        accumulate(right, c, False)

        for k in range(CHUNKS - 2):

            @pl.when(c == k + 2)
            def _(k=k):
                export_core(k)
                export_end(k)

        @pl.when(c >= 1)
        def _():
            export_start(c - 1)

        forward_arrival(0, c).wait_recv()
        forward_arrival(1, c).wait_recv()
        accumulate(opposite, c, False)

        scale = lax.rsqrt(squares[...] / width + norm_epsilon)
        cosine = angle_cos[c]
        sine = angle_sin[c]
        for head in range(cols // HD):
            at = pl.ds(head * HD, HD)
            value = acc[:, at] * scale
            if head * HD < q_cols + k_cols:
                value = value * cosine + pltpu.roll(value, HD // 2, 1) * sine
            made[:, :, at] = value.astype(jnp.bfloat16).reshape(nodes, TOK, HD)

        def fill(d, carry2):
            send[c, d] = made[index_sm[d]]
            return carry2

        lax.fori_loop(0, leafs, fill, 0)
        lax.fori_loop(1, leafs, lambda o, carry2: (slot_copy(o, c).start(), carry2)[1], 0)
        recv[c, me] = send[c, me]

        @pl.when(c + 1 < CHUNKS)
        def _():
            pass_on(c + 1)


        return carry

    lax.fori_loop(0, CHUNKS, one_chunk, 0)

    last = CHUNKS - 1
    export_core(last - 1)
    export_end(last - 1)
    attend(0, last, 0, last, False)
    export_start(last)
    attend(last, CHUNKS, 0, last, False)
    export_core(last)
    export_end(last)
    attend(0, CHUNKS, last, CHUNKS, True)

    def settle(c, carry):
        for side in (0, 1):
            full(side, 0, c).wait_send()
            full(side, 1, c).wait_send()
            forward(side, c).wait_send()
        sent = send.at[c, pl.ds(0, leafs - 1)]
        pltpu.make_async_copy(sent, sent, slot_send.at[c]).wait()
        exported = far.at[c, pl.ds(0, (chips - 1) * EXPORT)]
        pltpu.make_async_copy(exported, exported, chip_send.at[c]).wait()
        core_copy(c).wait_send()
        return carry

    lax.fori_loop(0, CHUNKS, settle, 0)
    pltpu.make_async_copy(ids_out.at[pl.ds(0, leafs - 1)], ids_out.at[pl.ds(0, leafs - 1)], ids_send).wait()


def on_device(tokens, norm_gain, w_query, w_key, w_value, gen_node, partition, parent, block_mask):
    leafs = lax.axis_size("leaf")
    nodes = gen_node.shape[0]
    feat = tokens.shape[1]
    width = norm_gain.shape[0]
    q_cols = w_query.shape[1]
    k_cols = w_key.shape[1]
    cols = q_cols + 2 * k_cols
    heads = k_cols // HD
    rows = nodes * TOK
    head_rows = q_cols // k_cols * NODE_TOK
    node_total = parent.shape[0]
    half_dim = HD // 2
    inverse_freq = np.exp(
        np.arange(half_dim, dtype=np.float32) * np.float32(-2.0 * math.log(rope_base) / HD)
    ).astype(np.float32)
    freq = jnp.asarray(np.concatenate([inverse_freq, inverse_freq])[None, :])
    bf16, f32, i32 = jnp.bfloat16, jnp.float32, jnp.int32
    dma = pltpu.SemaphoreType.DMA
    smem = pl.BlockSpec(memory_space=pltpu.SMEM)
    vmem = pl.BlockSpec(memory_space=pltpu.VMEM)
    hbm = pl.BlockSpec(memory_space=pl.ANY)
    out = pl.pallas_call(
        functools.partial(fused_kernel, leafs, nodes, width, q_cols, k_cols),
        out_shape=jax.ShapeDtypeStruct((SLOTS, NODE_TOK, q_cols), bf16),
        in_specs=[smem, smem, smem, vmem, vmem, vmem, hbm, hbm, hbm, hbm],
        out_specs=vmem,
        scratch_shapes=[
            pltpu.VMEM((4, CHUNKS, nodes, TOK, feat), bf16),
            pltpu.VMEM((4, feat, cols), bf16),
            pltpu.VMEM((rows, feat), bf16),
            pltpu.VMEM((rows, cols), f32),
            pltpu.VMEM((rows, 128), f32),
            pltpu.VMEM((CHUNKS, rows, HD), f32),
            pltpu.VMEM((CHUNKS, rows, HD), f32),
            pltpu.VMEM((nodes, TOK, cols), bf16),
            pltpu.VMEM((CHUNKS, leafs, TOK, cols), bf16),
            pltpu.VMEM((CHUNKS, leafs, TOK, cols), bf16),
            pltpu.VMEM((CHUNKS, leafs * EXPORT, TOK, 2 * k_cols), bf16),
            pltpu.VMEM((CHUNKS, leafs, TOK, q_cols), bf16),
            pltpu.VMEM((CHUNKS, leafs + leafs * EXPORT, TOK, 2 * k_cols), bf16),
            pltpu.VMEM((SLOTS, heads, head_rows, HD), f32),
            pltpu.VMEM((SLOTS, heads, head_rows, HD), f32),
            pltpu.VMEM((leafs, 8, 128), i32),
            pltpu.VMEM((leafs, 8, 128), i32),
            pltpu.VMEM((32, 128), i32),
            pltpu.VMEM((4, 1, feat), f32),
            pltpu.SMEM((node_total,), i32),
            pltpu.SMEM((leafs,), i32),
            pltpu.SMEM((leafs,), i32),
            pltpu.SMEM((leafs,), i32),
            pltpu.SMEM((32, 128), i32),
            pltpu.SMEM((SLOTS * ANC,), i32),
            dma((3,)),
            dma((CHUNKS,)),
            dma((2, 2, CHUNKS)),
            dma((2, 2, CHUNKS)),
            dma((2, CHUNKS)),
            dma((2, CHUNKS)),
            dma,
            dma,
            dma,
            dma((CHUNKS,)),
            dma((CHUNKS,)),
            dma((CHUNKS,)),
            dma((CHUNKS,)),
            dma((CHUNKS,)),
            dma((CHUNKS,)),
        ],
        compiler_params=pltpu.CompilerParams(
            collective_id=0, has_side_effects=True, vmem_limit_bytes=62 * 1024 * 1024
        ),
        cost_estimate=pl.CostEstimate(
            flops=2 * nodes * NODE_TOK * width * cols, bytes_accessed=30_000_000, transcendentals=0
        ),
        name="tree_attention",
    )(
        gen_node, partition, parent, block_mask, norm_gain, freq,
        tokens.reshape(nodes, NODE_TOK, feat),
        w_query.reshape(4, feat, q_cols), w_key.reshape(4, feat, k_cols), w_value.reshape(4, feat, k_cols),
    )
    return out.reshape(CAP * NODE_TOK, q_cols)


def solution(mesh):
    in_specs = (
        P("leaf", "mp"),
        P(),
        P(None, "mp"),
        P(None, "mp"),
        P(None, "mp"),
        P("leaf"),
        P(),
        P(),
        P(),
    )
    out_specs = P("leaf", "mp")
    return jax.shard_map(
        on_device, mesh=mesh, in_specs=in_specs, out_specs=out_specs, check_vma=False
    )
```

```python
import functools
import math

import jax
import jax.numpy as jnp
import numpy as np
from jax import lax
from jax.experimental import pallas as pl
from jax.experimental.pallas import tpu as pltpu
from jax.sharding import PartitionSpec as P

HD = 128
CAP = 31
ANC = 8
EXPORT = 2
CHUNKS = 4
NODE_TOK = 64
TOK = NODE_TOK // CHUNKS
SLOTS = CAP
BATCH = 8
CHIP_STEPS = [(2, 2), (0, 1), (1, 0), (0, 3), (3, 0), (2, 1), (1, 2), (2, 3), (3, 2), (0, 2), (2, 0), (1, 1), (3, 3), (1, 3), (3, 1)]
SLOT_STEPS = [(2, 2, 0), (0, 1, 0), (1, 0, 0), (0, 3, 0), (3, 0, 0), (2, 1, 0), (1, 2, 0), (2, 3, 0), (3, 2, 0), (0, 2, 0), (2, 0, 0), (1, 1, 0), (3, 3, 0), (1, 3, 0), (3, 1, 0), (2, 2, 1), (0, 1, 1), (1, 0, 1), (0, 3, 1), (3, 0, 1), (2, 1, 1), (1, 2, 1), (2, 3, 1), (3, 2, 1), (0, 2, 1), (2, 0, 1), (1, 1, 1), (3, 3, 1), (1, 3, 1), (3, 1, 1), (0, 0, 1)]

norm_epsilon = 1e-06
soft_cap = 50.0
query_scale = 144.0 ** (-0.5)
rope_base = 10000.0

MESH = pl.DeviceIdType.MESH


def fused_kernel(
    leafs, nodes, width, q_cols, k_cols,
    gen_ref, part_ref, parent_ref, mask_ref, gain_ref, freq_ref, tok_ref, wq_ref, wk_ref, wv_ref,
    out_ref,
    pieces, weights, scaled, acc, squares, angle_cos, angle_sin, made, send_kv, send_q, recv_kv, recv_q, far,
    query, pool, numer, total, ids_out, ids_in, table_vm, gain_vm,
    depth_sm, index_sm, start_sm, end_sm, table_sm, place_sm,
    load_sem, own_sem, full_send, full_recv, half_send, half_recv, ids_send, ids_recv, table_sem,
    kv_send, kv_recv, q_send, q_recv, chip_send, chip_recv, core_send, core_recv,
):
    me = lax.axis_index("leaf")
    z = lax.axis_index("mp")
    mp = 4
    right, left = lax.rem(z + 1, mp), lax.rem(z + 3, mp)
    opposite = lax.rem(z + 2, mp)
    feat = width // mp
    rows = nodes * TOK
    cols = q_cols + 2 * k_cols
    half = nodes // 2
    node_total = parent_ref.shape[0]
    core = lax.rem(me, 2)
    chip = lax.div(me, 2)
    chips = leafs // 2

    def chip_at(dy, dx):
        return lax.rem(lax.div(chip, 4) + dy, chips // 4) * 4 + lax.rem(lax.rem(chip, 4) + dx, 4)


    loads = [
        pltpu.make_async_copy(wq_ref, weights.at[:, :, pl.ds(0, q_cols)], load_sem.at[0]),
        pltpu.make_async_copy(wk_ref, weights.at[:, :, pl.ds(q_cols, k_cols)], load_sem.at[1]),
        pltpu.make_async_copy(wv_ref, weights.at[:, :, pl.ds(q_cols + k_cols, k_cols)], load_sem.at[2]),
    ]

    def own_load(c):
        return pltpu.make_async_copy(
            tok_ref.at[:, pl.ds(pl.multiple_of(c * TOK, TOK), TOK), :], pieces.at[z, c], own_sem.at[c]
        )

    barrier = pltpu.get_barrier_semaphore()

    def greet(o, carry):
        peer = lax.rem(me + o, leafs)
        pl.semaphore_signal(barrier, inc=1, device_id=(peer, z), device_id_type=MESH)
        return carry

    lax.fori_loop(1, leafs, greet, 0)
    pl.semaphore_signal(barrier, inc=1, device_id=(me, right), device_id_type=MESH)
    pl.semaphore_signal(barrier, inc=1, device_id=(me, left), device_id_type=MESH)
    for c in range(CHUNKS):
        own_load(c).start()
    for load in loads:
        load.start()
    pl.semaphore_wait(barrier, leafs + 1)

    def full(side, part, c):
        piece = pieces.at[z, c, pl.ds(part * half, half)]
        return pltpu.make_async_remote_copy(
            src_ref=piece,
            dst_ref=piece,
            send_sem=full_send.at[side, part, c],
            recv_sem=full_recv.at[side, part, c],
            device_id=(me, right if side == 0 else left),
            device_id_type=MESH,
        )

    def full_arrival(side, part, c):
        piece = pieces.at[left if side == 0 else right, c, pl.ds(part * half, half)]
        return pltpu.make_async_remote_copy(
            src_ref=piece,
            dst_ref=piece,
            send_sem=full_send.at[side, part, c],
            recv_sem=full_recv.at[side, part, c],
            device_id=(me, right if side == 0 else left),
            device_id_type=MESH,
        )

    def forward(side, c):
        source = left if side == 0 else right
        part = pieces.at[source, c, pl.ds(side * half, half)]
        return pltpu.make_async_remote_copy(
            src_ref=part,
            dst_ref=part,
            send_sem=half_send.at[side, c],
            recv_sem=half_recv.at[side, c],
            device_id=(me, right if side == 0 else left),
            device_id_type=MESH,
        )

    def forward_arrival(side, c):
        part = pieces.at[opposite, c, pl.ds(side * half, half)]
        return pltpu.make_async_remote_copy(
            src_ref=part,
            dst_ref=part,
            send_sem=half_send.at[side, c],
            recv_sem=half_recv.at[side, c],
            device_id=(me, right if side == 0 else left),
            device_id_type=MESH,
        )

    for c in range(CHUNKS):
        own_load(c).wait()
        if c == 0:
            for step in (0, 1):
                for side in (0, 1):
                    full(side, side ^ step, 0).start()

    def pass_on(c, between=None):
        for side in (0, 1):
            full_arrival(side, side, c).wait_recv()
            forward(side, c).start()

        @pl.when(c + 1 < CHUNKS)
        def _():
            for side in (0, 1):
                full(side, side, c + 1).start()

        if between is not None:
            between()
        for side in (0, 1):
            full_arrival(side, 1 - side, c).wait_recv()

        @pl.when(c + 1 < CHUNKS)
        def _():
            for side in (0, 1):
                full(side, 1 - side, c + 1).start()

    for part in range(mp):
        gain_vm[part] = gain_ref[pl.ds(part * feat, feat)].astype(jnp.float32).reshape(1, feat)

    def ranges(d, first):
        last = first + part_ref[d]
        start_sm[d] = first
        end_sm[d] = last
        found = jnp.int32(0)
        for b in range(nodes):
            node = gen_ref[b]
            found = found + jnp.where((node >= first) & (node < last), b + 1, 0)
        local = jnp.clip(found - 1, 0, nodes - 1)
        index_sm[d] = local
        ids_out[d] = jnp.full((8, 128), jnp.where(found > 0, gen_ref[local], -1), jnp.int32)
        return last

    lax.fori_loop(0, leafs, ranges, jnp.int32(0))

    def ids_copy(o):
        peer = lax.rem(me + o, leafs)
        return pltpu.make_async_remote_copy(
            src_ref=ids_out.at[peer],
            dst_ref=ids_in.at[me],
            send_sem=ids_send,
            recv_sem=ids_recv,
            device_id=(peer, z),
            device_id_type=MESH,
        )

    lax.fori_loop(1, leafs, lambda o, carry: (ids_copy(o).start(), carry)[1], 0)
    ids_in[me] = ids_out[me]

    depth_sm[0] = jnp.int32(0)

    def deeper(n, carry):
        depth_sm[n] = depth_sm[parent_ref[n]] + 1
        return carry

    lax.fori_loop(1, node_total, deeper, 0)

    pass_on(jnp.int32(0))

    token_row = lax.broadcasted_iota(jnp.int32, (TOK, HD), 0)
    sign = jnp.where(lax.broadcasted_iota(jnp.int32, (rows, HD), 1) < HD // 2, -1.0, 1.0)

    def tables(c, carry):
        def one_node(b, carry2):
            position = depth_sm[gen_ref[b]] * NODE_TOK + c * TOK + token_row
            at = pl.ds(pl.multiple_of(b * TOK, TOK), TOK)
            angle_cos[c, at, :] = position.astype(jnp.float32) * freq_ref[...]
            return carry2

        lax.fori_loop(0, nodes, one_node, 0)
        angles = angle_cos[c]
        angle_sin[c] = jnp.sin(angles) * sign
        angle_cos[c] = jnp.cos(angles)
        return carry

    lax.fori_loop(0, CHUNKS, tables, 0)

    lane8 = lax.broadcasted_iota(jnp.int32, (8, node_total), 1)

    def spans(step, carry):
        d = leafs - 1 - step
        end_of, start_of, owner = carry
        inside = lane8 < end_sm[d]
        return (
            jnp.where(inside, end_sm[d], end_of),
            jnp.where(inside, start_sm[d], start_of),
            jnp.where(inside, d, owner),
        )

    blank = jnp.zeros((8, node_total), jnp.int32)
    end_of, start_of, owner = lax.fori_loop(0, leafs, spans, (blank, blank, blank))
    my_start = start_sm[me]
    row_id = lax.broadcasted_iota(jnp.int32, (node_total, node_total), 0)
    col_id = lax.broadcasted_iota(jnp.int32, (node_total, node_total), 1)
    mask = mask_ref[...]
    foreign = (mask > 0) & (row_id >= end_of[0:1, :])
    seen = jnp.max(jnp.where(foreign, 1.0, 0.0), axis=0, keepdims=True)
    earlier = jnp.where((row_id < col_id) & (row_id >= start_of[0:1, :]), 1.0, 0.0).astype(jnp.bfloat16)
    seen8 = jnp.broadcast_to(seen, (8, node_total))
    rank8 = jnp.dot(seen8.astype(jnp.bfloat16), earlier, preferred_element_type=jnp.float32)
    owner_f = owner.astype(jnp.float32)
    core_f = lax.rem(owner, 2).astype(jnp.float32)
    chip_f = lax.div(owner, 2).astype(jnp.float32)
    far_place = leafs + core_f * leafs + chip_f * EXPORT + jnp.minimum(rank8, EXPORT - 1.0)
    relative = (lane8 - my_start).astype(jnp.float32)
    place = jnp.where(lane8 >= my_start, relative, far_place)

    slot_row = lax.broadcasted_iota(jnp.int32, (32, node_total), 0)
    slot_col = lax.broadcasted_iota(jnp.int32, (32, node_total), 1)
    own_here = slot_col == my_start + slot_row
    own_mask = jnp.dot(
        jnp.where(own_here, 1.0, 0.0).astype(jnp.bfloat16),
        jnp.where(mask > 0, 1.0, 0.0).astype(jnp.bfloat16),
        preferred_element_type=jnp.float32,
    )
    others = jnp.where((own_mask > 0.5) & ~own_here, 1.0, 0.0)
    before = jnp.where(row_id < col_id, 1.0, 0.0).astype(jnp.bfloat16)
    rank = jnp.dot(others.astype(jnp.bfloat16), before, preferred_element_type=jnp.float32)
    lane32 = lax.broadcasted_iota(jnp.int32, (32, 128), 1)
    row32 = lax.broadcasted_iota(jnp.int32, (32, 128), 0)
    table = jnp.zeros((32, 128), jnp.float32)
    for r in range(ANC - 1):
        hit = (others > 0.5) & (jnp.abs(rank - float(r)) < 0.5)
        value = jnp.sum(jnp.where(hit, place[0:1, :], 0.0), axis=1, keepdims=True)
        table = jnp.where(lane32 == r, value, table)
    table = jnp.where(lane32 == ANC - 1, jnp.sum(others, axis=1, keepdims=True), table)

    pltpu.make_async_copy(ids_in.at[pl.ds(0, leafs - 1)], ids_in.at[pl.ds(0, leafs - 1)], ids_recv).wait()

    def sources(s, total):
        return total + jnp.where(ids_in[s][0:1, :] == my_start + row32, s.astype(jnp.float32), 0.0)

    source = lax.fori_loop(0, leafs, sources, jnp.zeros((32, 128), jnp.float32))
    table = jnp.where(lane32 == 2 * ANC, source, table)
    mine8 = (lane8 >= my_start) & (owner == me) & (seen8 > 0.5)
    for k in range(EXPORT):
        picked = jnp.sum(
            jnp.where(mine8 & (jnp.abs(rank8 - float(k)) < 0.5), relative, 0.0), axis=1, keepdims=True
        )
        chosen = jnp.sum(
            jnp.where(row32.astype(jnp.float32) == picked[0:1, :], source, 0.0), axis=0, keepdims=True
        )
        table = jnp.where(lane32 == 2 * ANC + 1 + k, chosen, table)
    table_vm[...] = table.astype(jnp.int32)
    to_scalars = pltpu.make_async_copy(table_vm, table_sm, table_sem)
    to_scalars.start()
    to_scalars.wait()

    def find_places(r, carry):
        place_sm[r * ANC] = jnp.clip(table_sm[r, 2 * ANC], 0, leafs - 1)
        for p in range(ANC - 1):
            v = table_sm[r, p]
            near = table_sm[jnp.clip(v, 0, leafs - 1), 2 * ANC]
            place_sm[r * ANC + p + 1] = jnp.clip(jnp.where(v < leafs, near, v), 0, leafs + leafs * EXPORT - 1)
        return carry

    lax.fori_loop(0, SLOTS, find_places, 0)
    my_count = part_ref[me]

    for load in loads:
        load.wait()
    def accumulate(src, c, first):
        wide = pieces[src, c].reshape(rows, feat).astype(jnp.float32)
        gain = gain_vm[src]
        scaled[...] = (wide * gain).astype(jnp.bfloat16)
        part = jnp.sum(wide * wide, axis=1, keepdims=True)
        if first:
            squares[...] = jnp.broadcast_to(part, (rows, 128))
        else:
            squares[...] += jnp.broadcast_to(part, (rows, 128))
        if src is opposite:
            return
        product = jnp.dot(scaled[...], weights[src], preferred_element_type=jnp.float32)
        if first:
            acc[...] = product
        else:
            acc[...] += product

    def slot_copy(step, c, source, target, sent, arrived):
        peer = chip_at(step[0], step[1]) * 2 + lax.rem(core + step[2], 2)
        return pltpu.make_async_remote_copy(
            src_ref=source.at[c, peer],
            dst_ref=target.at[c, me],
            send_sem=sent.at[c],
            recv_sem=arrived.at[c],
            device_id=(peer, z),
            device_id_type=MESH,
        )

    def all_slots(buffer, c, sem):
        part = buffer.at[c, pl.ds(0, leafs - 1)]
        pltpu.make_async_copy(part, part, sem.at[c]).wait()

    block = core * chips * EXPORT + chip * EXPORT

    def chip_copy(step, c):
        part = far.at[c, pl.ds(block, EXPORT)]
        return pltpu.make_async_remote_copy(
            src_ref=part, dst_ref=part, send_sem=chip_send.at[c], recv_sem=chip_recv.at[c],
            device_id=(chip_at(step[0], step[1]) * 2 + core, z), device_id_type=MESH,
        )

    def chips_arrived(c):
        part = far.at[c, pl.ds(0, (chips - 1) * EXPORT)]
        pltpu.make_async_copy(part, part, chip_recv.at[c]).wait()

    def core_copy(c):
        part = far.at[c, pl.ds(core * chips * EXPORT, chips * EXPORT)]
        return pltpu.make_async_remote_copy(
            src_ref=part, dst_ref=part, send_sem=core_send.at[c], recv_sem=core_recv.at[c],
            device_id=(chip * 2 + 1 - core, z), device_id_type=MESH,
        )

    def core_arrival(c):
        part = far.at[c, pl.ds((1 - core) * chips * EXPORT, chips * EXPORT)]
        return pltpu.make_async_remote_copy(
            src_ref=part, dst_ref=part, send_sem=core_send.at[c], recv_sem=core_recv.at[c],
            device_id=(chip * 2 + 1 - core, z), device_id_type=MESH,
        )

    kv_cols = 2 * k_cols

    def export_start(c):
        all_slots(recv_kv, c, kv_recv)

        def keep(i, carry):
            for n in range(4):
                pool[c, i * 4 + n] = recv_kv[c, i * 4 + n]
            return carry

        lax.fori_loop(0, leafs // 4, keep, 0)
        for k in range(EXPORT):
            far[c, block + k] = pool[c, jnp.clip(table_sm[0, 2 * ANC + 1 + k], 0, leafs - 1)]
        for step in CHIP_STEPS:
            chip_copy(step, c).start()

    def keep_queries(c):
        all_slots(recv_q, c, q_recv)

        def keep(i, carry):
            for n in range(4):
                query[c, i * 4 + n] = recv_q[c, i * 4 + n]
            return carry

        lax.fori_loop(0, leafs // 4, keep, 0)

    def export_core(c):
        chips_arrived(c)
        core_copy(c).start()

    def export_end(c):
        core_arrival(c).wait_recv()

        def keep(i, carry):
            for n in range(4):
                pool[c, leafs + i * 4 + n] = far[c, i * 4 + n]
            return carry

        lax.fori_loop(0, leafs * EXPORT // 4, keep, 0)

    heads = k_cols // HD
    groups = q_cols // k_cols
    q_rows = groups * TOK
    lane = lax.broadcasted_iota(jnp.int32, (1, ANC * TOK), 1)

    tri = lax.broadcasted_iota(jnp.int32, (q_rows, ANC * TOK), 1) <= lax.rem(
        lax.broadcasted_iota(jnp.int32, (q_rows, ANC * TOK), 0), TOK
    )
    tri = tri | (lax.broadcasted_iota(jnp.int32, (q_rows, ANC * TOK), 1) >= TOK)

    def load_queries(own, h, first, last):
        return jnp.concatenate(
            [
                query[c, own, :, pl.ds((h * groups + g) * HD, HD)]
                for c in range(first, last)
                for g in range(groups)
            ],
            axis=0,
        )

    def load_pool(places, column, first, last):
        return jnp.concatenate(
            [pool[c, p, :, pl.ds(column, HD)] for c in range(first, last) for p in places], axis=0
        )

    def attend(q0, q1, k0, k1, final):
        at = pl.ds(q0 * q_rows, (q1 - q0) * q_rows)

        def batch(slots):
            chains = [(n, h) for n in range(len(slots)) for h in range(heads)]
            places = [[place_sm[r * ANC + p] for p in range(ANC)] for r in slots]
            limit = [lane < (table_sm[r, ANC - 1] + 1) * TOK for r in slots]
            past = [x & (lane >= TOK) for x in limit]
            scores = {
                (n, h): lax.dot_general(
                    load_queries(places[n][0], h, q0, q1),
                    load_pool(places[n], h * HD, k0, k1),
                    (((1,), (1,)), ((), ())),
                    preferred_element_type=jnp.float32,
                )
                for n, h in chains
            }
            probs, sums = {}, {}
            for n, h in chains:
                capped = jnp.tanh(scores[n, h] * (query_scale / soft_cap))
                raised = jnp.exp2(capped * (soft_cap * math.log2(math.e)))
                lines, adds = [], []
                for q in range(q0, q1):
                    tiles = []
                    for k in range(k0, k1):
                        tile = raised[
                            (q - q0) * q_rows : (q - q0 + 1) * q_rows,
                            (k - k0) * ANC * TOK : (k - k0 + 1) * ANC * TOK,
                        ]
                        keep = limit[n] if k < q else past[n] if k > q else limit[n] & tri
                        tiles.append(jnp.where(keep, tile, 0.0))
                    lines.append(jnp.concatenate(tiles, axis=1))
                    adds.append(functools.reduce(lambda x, y: x + y, tiles))
                probs[n, h] = jnp.concatenate(lines, axis=0).astype(jnp.bfloat16)
                sums[n, h] = jnp.concatenate(adds, axis=0)
            parts = {
                (n, h): jnp.dot(
                    probs[n, h],
                    load_pool(places[n], k_cols + h * HD, k0, k1),
                    preferred_element_type=jnp.float32,
                )
                for n, h in chains
            }
            if not final:
                for n, h in chains:
                    numer[slots[n], h, at, :] = parts[n, h]
                    total[slots[n], h, at, :] = sums[n, h]
                return
            results = {}
            for n, h in chains:
                whole = jnp.sum(total[slots[n], h] + sums[n, h], axis=1, keepdims=True)
                result = (numer[slots[n], h] + parts[n, h]) * (1.0 / whole)
                results[n, h] = jnp.where(slots[n] < my_count, result, 0.0).astype(jnp.bfloat16)
            for n, h in chains:
                for q in range(CHUNKS):
                    for g in range(groups):
                        start = (q * groups + g) * TOK
                        out_ref[slots[n], pl.ds(q * TOK, TOK), pl.ds((h * groups + g) * HD, HD)] = results[n, h][
                            start : start + TOK
                        ]

        def step(i, carry):
            batch([i * BATCH + n for n in range(BATCH)])
            return carry

        lax.fori_loop(0, SLOTS // BATCH, step, 0)
        if SLOTS % BATCH:
            batch(list(range(SLOTS // BATCH * BATCH, SLOTS)))

    def one_chunk(c, carry):
        accumulate(z, c, True)
        accumulate(left, c, False)
        accumulate(right, c, False)

        for k in range(CHUNKS - 2):

            @pl.when(c == k + 2)
            def _(k=k):
                export_core(k)
                export_end(k)

        @pl.when(c >= 1)
        def _():
            keep_queries(c - 1)

        forward_arrival(0, c).wait_recv()
        forward_arrival(1, c).wait_recv()
        accumulate(opposite, c, False)

        scale = lax.rsqrt(squares[...] / width + norm_epsilon)
        cosine = angle_cos[c]
        sine = angle_sin[c]

        def finish(first, count, target, buffer, sent, arrived):
            at = pl.ds(first, count)
            acc[:, at] += jnp.dot(scaled[...], weights[opposite, :, at], preferred_element_type=jnp.float32)
            for column in range(first, first + count, HD):
                value = acc[:, pl.ds(column, HD)] * scale
                if column < q_cols + k_cols:
                    value = value * cosine + pltpu.roll(value, HD // 2, 1) * sine
                made[:, :, pl.ds(column, HD)] = value.astype(jnp.bfloat16).reshape(nodes, TOK, HD)

            def fill(i, carry2):
                for n in range(4):
                    d = i * 4 + n
                    target[c, d] = made[index_sm[d], :, at]
                return carry2

            lax.fori_loop(0, leafs // 4, fill, 0)
            for step in SLOT_STEPS:
                slot_copy(step, c, target, buffer, sent, arrived).start()
            buffer[c, me] = target[c, me]

        finish(q_cols, 2 * k_cols, send_kv, recv_kv, kv_send, kv_recv)
        finish(0, q_cols, send_q, recv_q, q_send, q_recv)

        @pl.when(c + 1 < CHUNKS)
        def _():
            pass_on(c + 1, lambda: export_start(c))

        return carry

    lax.fori_loop(0, CHUNKS, one_chunk, 0)

    last = CHUNKS - 1
    export_core(last - 1)
    export_end(last - 1)
    attend(0, last, 0, last, False)
    export_start(last)
    keep_queries(last)
    attend(last, CHUNKS, 0, last, False)
    export_core(last)
    export_end(last)
    attend(0, CHUNKS, last, CHUNKS, True)

    def settle(c, carry):
        for side in (0, 1):
            full(side, 0, c).wait_send()
            full(side, 1, c).wait_send()
            forward(side, c).wait_send()
        all_slots(send_kv, c, kv_send)
        all_slots(send_q, c, q_send)
        exported = far.at[c, pl.ds(0, (chips - 1) * EXPORT)]
        pltpu.make_async_copy(exported, exported, chip_send.at[c]).wait()
        core_copy(c).wait_send()
        return carry

    lax.fori_loop(0, CHUNKS, settle, 0)
    pltpu.make_async_copy(ids_out.at[pl.ds(0, leafs - 1)], ids_out.at[pl.ds(0, leafs - 1)], ids_send).wait()


def on_device(tokens, norm_gain, w_query, w_key, w_value, gen_node, partition, parent, block_mask):
    leafs = lax.axis_size("leaf")
    nodes = gen_node.shape[0]
    feat = tokens.shape[1]
    width = norm_gain.shape[0]
    q_cols = w_query.shape[1]
    k_cols = w_key.shape[1]
    cols = q_cols + 2 * k_cols
    heads = k_cols // HD
    rows = nodes * TOK
    head_rows = q_cols // k_cols * NODE_TOK
    node_total = parent.shape[0]
    half_dim = HD // 2
    inverse_freq = np.exp(
        np.arange(half_dim, dtype=np.float32) * np.float32(-2.0 * math.log(rope_base) / HD)
    ).astype(np.float32)
    freq = jnp.asarray(np.concatenate([inverse_freq, inverse_freq])[None, :])
    bf16, f32, i32 = jnp.bfloat16, jnp.float32, jnp.int32
    dma = pltpu.SemaphoreType.DMA
    smem = pl.BlockSpec(memory_space=pltpu.SMEM)
    vmem = pl.BlockSpec(memory_space=pltpu.VMEM)
    hbm = pl.BlockSpec(memory_space=pl.ANY)
    out = pl.pallas_call(
        functools.partial(fused_kernel, leafs, nodes, width, q_cols, k_cols),
        out_shape=jax.ShapeDtypeStruct((SLOTS, NODE_TOK, q_cols), bf16),
        in_specs=[smem, smem, smem, vmem, vmem, vmem, hbm, hbm, hbm, hbm],
        out_specs=vmem,
        scratch_shapes=[
            pltpu.VMEM((4, CHUNKS, nodes, TOK, feat), bf16),
            pltpu.VMEM((4, feat, cols), bf16),
            pltpu.VMEM((rows, feat), bf16),
            pltpu.VMEM((rows, cols), f32),
            pltpu.VMEM((rows, 128), f32),
            pltpu.VMEM((CHUNKS, rows, HD), f32),
            pltpu.VMEM((CHUNKS, rows, HD), f32),
            pltpu.VMEM((nodes, TOK, cols), bf16),
            pltpu.VMEM((CHUNKS, leafs, TOK, 2 * k_cols), bf16),
            pltpu.VMEM((CHUNKS, leafs, TOK, q_cols), bf16),
            pltpu.VMEM((CHUNKS, leafs, TOK, 2 * k_cols), bf16),
            pltpu.VMEM((CHUNKS, leafs, TOK, q_cols), bf16),
            pltpu.VMEM((CHUNKS, leafs * EXPORT, TOK, 2 * k_cols), bf16),
            pltpu.VMEM((CHUNKS, leafs, TOK, q_cols), bf16),
            pltpu.VMEM((CHUNKS, leafs + leafs * EXPORT, TOK, 2 * k_cols), bf16),
            pltpu.VMEM((SLOTS, heads, head_rows, HD), f32),
            pltpu.VMEM((SLOTS, heads, head_rows, HD), f32),
            pltpu.VMEM((leafs, 8, 128), i32),
            pltpu.VMEM((leafs, 8, 128), i32),
            pltpu.VMEM((32, 128), i32),
            pltpu.VMEM((4, 1, feat), f32),
            pltpu.SMEM((node_total,), i32),
            pltpu.SMEM((leafs,), i32),
            pltpu.SMEM((leafs,), i32),
            pltpu.SMEM((leafs,), i32),
            pltpu.SMEM((32, 128), i32),
            pltpu.SMEM((SLOTS * ANC,), i32),
            dma((3,)),
            dma((CHUNKS,)),
            dma((2, 2, CHUNKS)),
            dma((2, 2, CHUNKS)),
            dma((2, CHUNKS)),
            dma((2, CHUNKS)),
            dma,
            dma,
            dma,
            dma((CHUNKS,)),
            dma((CHUNKS,)),
            dma((CHUNKS,)),
            dma((CHUNKS,)),
            dma((CHUNKS,)),
            dma((CHUNKS,)),
            dma((CHUNKS,)),
            dma((CHUNKS,)),
        ],
        compiler_params=pltpu.CompilerParams(
            collective_id=0, has_side_effects=True, vmem_limit_bytes=62 * 1024 * 1024
        ),
        cost_estimate=pl.CostEstimate(
            flops=2 * nodes * NODE_TOK * width * cols, bytes_accessed=30_000_000, transcendentals=0
        ),
        name="tree_attention",
    )(
        gen_node, partition, parent, block_mask, norm_gain, freq,
        tokens.reshape(nodes, NODE_TOK, feat),
        w_query.reshape(4, feat, q_cols), w_key.reshape(4, feat, k_cols), w_value.reshape(4, feat, k_cols),
    )
    return out.reshape(CAP * NODE_TOK, q_cols)


def solution(mesh):
    in_specs = (
        P("leaf", "mp"),
        P(),
        P(None, "mp"),
        P(None, "mp"),
        P(None, "mp"),
        P("leaf"),
        P(),
        P(),
        P(),
    )
    out_specs = P("leaf", "mp")
    return jax.shard_map(
        on_device, mesh=mesh, in_specs=in_specs, out_specs=out_specs, check_vma=False
    )
```

```python
import functools
import math

import jax
import jax.numpy as jnp
import numpy as np
from jax import lax
from jax.experimental import pallas as pl
from jax.experimental.pallas import tpu as pltpu
from jax.sharding import PartitionSpec as P

HD = 128
CAP = 31
ANC = 8
EXPORT = 2
CHUNKS = 4
NODE_TOK = 64
TOK = NODE_TOK // CHUNKS
SUBS = 2 * CHUNKS
SUB = TOK // 2
SLOTS = CAP
BATCH = 8
OUT_PARTS = 8
CHIP_STEPS = [(2, 2), (0, 1), (1, 0), (0, 3), (3, 0), (2, 1), (1, 2), (2, 3), (3, 2), (0, 2), (2, 0), (1, 1), (3, 3), (1, 3), (3, 1)]
SLOT_STEPS = [(2, 2, 0), (0, 1, 0), (1, 0, 0), (0, 3, 0), (3, 0, 0), (2, 1, 0), (1, 2, 0), (2, 3, 0), (3, 2, 0), (0, 2, 0), (2, 0, 0), (1, 1, 0), (3, 3, 0), (1, 3, 0), (3, 1, 0), (2, 2, 1), (0, 1, 1), (1, 0, 1), (0, 3, 1), (3, 0, 1), (2, 1, 1), (1, 2, 1), (2, 3, 1), (3, 2, 1), (0, 2, 1), (2, 0, 1), (1, 1, 1), (3, 3, 1), (1, 3, 1), (3, 1, 1), (0, 0, 1)]

norm_epsilon = 1e-06
soft_cap = 50.0
query_scale = 144.0 ** (-0.5)
rope_base = 10000.0

MESH = pl.DeviceIdType.MESH


def fused_kernel(
    leafs, nodes, width, q_cols, k_cols,
    gen_ref, part_ref, parent_ref, mask_ref, gain_ref, freq_ref, tok_ref, wq_ref, wk_ref, wv_ref,
    out_ref,
    held, pieces, weights, scaled, acc, squares, angle_cos, angle_sin, made, send, recv, near, far,
    query, pool, numer, total, ids_out, ids_in, table_vm, gain_vm,
    depth_sm, index_sm, start_sm, end_sm, table_sm, place_sm,
    load_sem, own_sem, full_send, full_recv, half_send, half_recv, ids_send, ids_recv, table_sem,
    slot_send, slot_recv, chip_send, chip_recv, core_send, core_recv,
):
    me = lax.axis_index("leaf")
    z = lax.axis_index("mp")
    mp = 4
    right, left = lax.rem(z + 1, mp), lax.rem(z + 3, mp)
    opposite = lax.rem(z + 2, mp)
    feat = width // mp
    rows = nodes * SUB
    cols = q_cols + 2 * k_cols
    half = nodes // 4
    node_total = parent_ref.shape[0]
    core = lax.rem(me, 2)
    chip = lax.div(me, 2)
    chips = leafs // 2

    def chip_at(dy, dx):
        return lax.rem(lax.div(chip, 4) + dy, chips // 4) * 4 + lax.rem(lax.rem(chip, 4) + dx, 4)


    loads = [
        pltpu.make_async_copy(wq_ref, weights.at[:, :, pl.ds(0, q_cols)], load_sem.at[0]),
        pltpu.make_async_copy(wk_ref, weights.at[:, :, pl.ds(q_cols, k_cols)], load_sem.at[1]),
        pltpu.make_async_copy(wv_ref, weights.at[:, :, pl.ds(q_cols + k_cols, k_cols)], load_sem.at[2]),
    ]

    def own_load(c):
        at = pl.ds(pl.multiple_of(c * TOK, TOK), TOK)
        return pltpu.make_async_copy(tok_ref.at[:, at, :], held.at[:, at, :], own_sem.at[c])

    def deal(c):
        at = pl.ds(pl.multiple_of(c * TOK, TOK), TOK)

        def pair(j, carry):
            one = held[2 * j, at, :].astype(jnp.float32)
            two = held[2 * j + 1, at, :].astype(jnp.float32)
            pieces[z, 2 * c, j] = jnp.concatenate([one[:SUB], two[:SUB]], axis=0).astype(jnp.bfloat16)
            pieces[z, 2 * c + 1, j] = jnp.concatenate([one[SUB:], two[SUB:]], axis=0).astype(jnp.bfloat16)
            return carry

        lax.fori_loop(0, nodes // 2, pair, 0)

    barrier = pltpu.get_barrier_semaphore()

    def greet(o, carry):
        peer = lax.rem(me + o, leafs)
        pl.semaphore_signal(barrier, inc=1, device_id=(peer, z), device_id_type=MESH)
        return carry

    lax.fori_loop(1, leafs, greet, 0)
    pl.semaphore_signal(barrier, inc=1, device_id=(me, right), device_id_type=MESH)
    pl.semaphore_signal(barrier, inc=1, device_id=(me, left), device_id_type=MESH)
    for c in range(CHUNKS):
        own_load(c).start()
    for load in loads:
        load.start()
    pl.semaphore_wait(barrier, leafs + 1)

    def full(side, part, c):
        piece = pieces.at[z, c, pl.ds(part * half, half)]
        return pltpu.make_async_remote_copy(
            src_ref=piece,
            dst_ref=piece,
            send_sem=full_send.at[side, part, c],
            recv_sem=full_recv.at[side, part, c],
            device_id=(me, right if side == 0 else left),
            device_id_type=MESH,
        )

    def full_arrival(side, part, c):
        piece = pieces.at[left if side == 0 else right, c, pl.ds(part * half, half)]
        return pltpu.make_async_remote_copy(
            src_ref=piece,
            dst_ref=piece,
            send_sem=full_send.at[side, part, c],
            recv_sem=full_recv.at[side, part, c],
            device_id=(me, right if side == 0 else left),
            device_id_type=MESH,
        )

    def forward(side, c):
        source = left if side == 0 else right
        part = pieces.at[source, c, pl.ds(side * half, half)]
        return pltpu.make_async_remote_copy(
            src_ref=part,
            dst_ref=part,
            send_sem=half_send.at[side, c],
            recv_sem=half_recv.at[side, c],
            device_id=(me, right if side == 0 else left),
            device_id_type=MESH,
        )

    def forward_arrival(side, c):
        part = pieces.at[opposite, c, pl.ds(side * half, half)]
        return pltpu.make_async_remote_copy(
            src_ref=part,
            dst_ref=part,
            send_sem=half_send.at[side, c],
            recv_sem=half_recv.at[side, c],
            device_id=(me, right if side == 0 else left),
            device_id_type=MESH,
        )

    for c in range(CHUNKS):
        own_load(c).wait()
    for c in range(CHUNKS):
        deal(c)
        if c == 0:
            for step in (0, 1):
                for side in (0, 1):
                    full(side, side ^ step, 0).start()

    def pass_on(c, between=None):
        for side in (0, 1):
            full_arrival(side, side, c).wait_recv()
            forward(side, c).start()

        @pl.when(c + 1 < SUBS)
        def _():
            for side in (0, 1):
                full(side, side, c + 1).start()

        if between is not None:
            between()
        for side in (0, 1):
            full_arrival(side, 1 - side, c).wait_recv()

        @pl.when(c + 1 < SUBS)
        def _():
            for side in (0, 1):
                full(side, 1 - side, c + 1).start()

    for part in range(mp):
        gain_vm[part] = gain_ref[pl.ds(part * feat, feat)].astype(jnp.float32).reshape(1, feat)

    def ranges(d, first):
        last = first + part_ref[d]
        start_sm[d] = first
        end_sm[d] = last
        found = jnp.int32(0)
        for b in range(nodes):
            node = gen_ref[b]
            found = found + jnp.where((node >= first) & (node < last), b + 1, 0)
        local = jnp.clip(found - 1, 0, nodes - 1)
        index_sm[d] = local
        ids_out[d] = jnp.full((8, 128), jnp.where(found > 0, gen_ref[local], -1), jnp.int32)
        return last

    lax.fori_loop(0, leafs, ranges, jnp.int32(0))

    def ids_copy(o):
        peer = lax.rem(me + o, leafs)
        return pltpu.make_async_remote_copy(
            src_ref=ids_out.at[peer],
            dst_ref=ids_in.at[me],
            send_sem=ids_send,
            recv_sem=ids_recv,
            device_id=(peer, z),
            device_id_type=MESH,
        )

    lax.fori_loop(1, leafs, lambda o, carry: (ids_copy(o).start(), carry)[1], 0)
    ids_in[me] = ids_out[me]

    depth_sm[0] = jnp.int32(0)

    def deeper(n, carry):
        depth_sm[n] = depth_sm[parent_ref[n]] + 1
        return carry

    lax.fori_loop(1, node_total, deeper, 0)

    pass_on(jnp.int32(0))

    token_row = lax.broadcasted_iota(jnp.int32, (SUB, HD), 0)
    sign = jnp.where(lax.broadcasted_iota(jnp.int32, (rows, HD), 1) < HD // 2, -1.0, 1.0)

    def tables(c, carry):
        def one_node(b, carry2):
            position = depth_sm[gen_ref[b]] * NODE_TOK + c * SUB + token_row
            at = pl.ds(pl.multiple_of(b * SUB, SUB), SUB)
            angle_cos[c, at, :] = position.astype(jnp.float32) * freq_ref[...]
            return carry2

        lax.fori_loop(0, nodes, one_node, 0)
        angles = angle_cos[c]
        angle_sin[c] = jnp.sin(angles) * sign
        angle_cos[c] = jnp.cos(angles)
        return carry

    lax.fori_loop(0, SUBS, tables, 0)

    lane8 = lax.broadcasted_iota(jnp.int32, (8, node_total), 1)

    def spans(step, carry):
        d = leafs - 1 - step
        end_of, start_of, owner = carry
        inside = lane8 < end_sm[d]
        return (
            jnp.where(inside, end_sm[d], end_of),
            jnp.where(inside, start_sm[d], start_of),
            jnp.where(inside, d, owner),
        )

    blank = jnp.zeros((8, node_total), jnp.int32)
    end_of, start_of, owner = lax.fori_loop(0, leafs, spans, (blank, blank, blank))
    my_start = start_sm[me]
    row_id = lax.broadcasted_iota(jnp.int32, (node_total, node_total), 0)
    col_id = lax.broadcasted_iota(jnp.int32, (node_total, node_total), 1)
    mask = mask_ref[...]
    foreign = (mask > 0) & (row_id >= end_of[0:1, :])
    seen = jnp.max(jnp.where(foreign, 1.0, 0.0), axis=0, keepdims=True)
    earlier = jnp.where((row_id < col_id) & (row_id >= start_of[0:1, :]), 1.0, 0.0).astype(jnp.bfloat16)
    seen8 = jnp.broadcast_to(seen, (8, node_total))
    rank8 = jnp.dot(seen8.astype(jnp.bfloat16), earlier, preferred_element_type=jnp.float32)
    owner_f = owner.astype(jnp.float32)
    core_f = lax.rem(owner, 2).astype(jnp.float32)
    chip_f = lax.div(owner, 2).astype(jnp.float32)
    far_place = leafs + core_f * leafs + chip_f * EXPORT + jnp.minimum(rank8, EXPORT - 1.0)
    relative = (lane8 - my_start).astype(jnp.float32)
    place = jnp.where(lane8 >= my_start, relative, far_place)

    slot_row = lax.broadcasted_iota(jnp.int32, (32, node_total), 0)
    slot_col = lax.broadcasted_iota(jnp.int32, (32, node_total), 1)
    own_here = slot_col == my_start + slot_row
    own_mask = jnp.dot(
        jnp.where(own_here, 1.0, 0.0).astype(jnp.bfloat16),
        jnp.where(mask > 0, 1.0, 0.0).astype(jnp.bfloat16),
        preferred_element_type=jnp.float32,
    )
    others = jnp.where((own_mask > 0.5) & ~own_here, 1.0, 0.0)
    before = jnp.where(row_id < col_id, 1.0, 0.0).astype(jnp.bfloat16)
    rank = jnp.dot(others.astype(jnp.bfloat16), before, preferred_element_type=jnp.float32)
    lane32 = lax.broadcasted_iota(jnp.int32, (32, 128), 1)
    row32 = lax.broadcasted_iota(jnp.int32, (32, 128), 0)
    table = jnp.zeros((32, 128), jnp.float32)
    for r in range(ANC - 1):
        hit = (others > 0.5) & (jnp.abs(rank - float(r)) < 0.5)
        value = jnp.sum(jnp.where(hit, place[0:1, :], 0.0), axis=1, keepdims=True)
        table = jnp.where(lane32 == r, value, table)
    table = jnp.where(lane32 == ANC - 1, jnp.sum(others, axis=1, keepdims=True), table)

    pltpu.make_async_copy(ids_in.at[pl.ds(0, leafs - 1)], ids_in.at[pl.ds(0, leafs - 1)], ids_recv).wait()

    def sources(s, total):
        return total + jnp.where(ids_in[s][0:1, :] == my_start + row32, s.astype(jnp.float32), 0.0)

    source = lax.fori_loop(0, leafs, sources, jnp.zeros((32, 128), jnp.float32))
    table = jnp.where(lane32 == 2 * ANC, source, table)
    mine8 = (lane8 >= my_start) & (owner == me) & (seen8 > 0.5)
    for k in range(EXPORT):
        picked = jnp.sum(
            jnp.where(mine8 & (jnp.abs(rank8 - float(k)) < 0.5), relative, 0.0), axis=1, keepdims=True
        )
        chosen = jnp.sum(
            jnp.where(row32.astype(jnp.float32) == picked[0:1, :], source, 0.0), axis=0, keepdims=True
        )
        table = jnp.where(lane32 == 2 * ANC + 1 + k, chosen, table)
    table_vm[...] = table.astype(jnp.int32)
    to_scalars = pltpu.make_async_copy(table_vm, table_sm, table_sem)
    to_scalars.start()
    to_scalars.wait()

    def find_places(r, carry):
        place_sm[r * ANC] = jnp.clip(table_sm[r, 2 * ANC], 0, leafs - 1)
        for p in range(ANC - 1):
            v = table_sm[r, p]
            near = table_sm[jnp.clip(v, 0, leafs - 1), 2 * ANC]
            place_sm[r * ANC + p + 1] = jnp.clip(jnp.where(v < leafs, near, v), 0, leafs + leafs * EXPORT - 1)
        return carry

    lax.fori_loop(0, SLOTS, find_places, 0)
    my_count = part_ref[me]

    for load in loads:
        load.wait()
    def accumulate(src, c, first):
        wide = pieces[src, c].reshape(rows, feat).astype(jnp.float32)
        gain = gain_vm[src]
        scaled[...] = (wide * gain).astype(jnp.bfloat16)
        part = jnp.sum(wide * wide, axis=1, keepdims=True)
        if first:
            squares[...] = jnp.broadcast_to(part, (rows, 128))
        else:
            squares[...] += jnp.broadcast_to(part, (rows, 128))
        if src is opposite:
            return
        product = jnp.dot(scaled[...], weights[src], preferred_element_type=jnp.float32)
        if first:
            acc[...] = product
        else:
            acc[...] += product

    def slot_copy(step, c):
        peer = chip_at(step[0], step[1]) * 2 + lax.rem(core + step[2], 2)
        return pltpu.make_async_remote_copy(
            src_ref=send.at[c, peer],
            dst_ref=recv.at[c, me],
            send_sem=slot_send.at[c],
            recv_sem=slot_recv.at[c],
            device_id=(peer, z),
            device_id_type=MESH,
        )

    def all_slots(buffer, c, sem):
        part = buffer.at[c, pl.ds(0, leafs - 1)]
        pltpu.make_async_copy(part, part, sem.at[c]).wait()

    place = core * chips + chip

    def chip_copy(step, c):
        part = far.at[c, place]
        return pltpu.make_async_remote_copy(
            src_ref=part, dst_ref=part, send_sem=chip_send.at[c], recv_sem=chip_recv.at[c],
            device_id=(chip_at(step[0], step[1]) * 2 + core, z), device_id_type=MESH,
        )

    def chips_arrived(c):
        part = far.at[c, pl.ds(0, chips - 1)]
        pltpu.make_async_copy(part, part, chip_recv.at[c]).wait()

    def core_copy(c):
        part = far.at[c, pl.ds(core * chips, chips)]
        return pltpu.make_async_remote_copy(
            src_ref=part, dst_ref=part, send_sem=core_send.at[c], recv_sem=core_recv.at[c],
            device_id=(chip * 2 + 1 - core, z), device_id_type=MESH,
        )

    def core_arrival(c):
        part = far.at[c, pl.ds((1 - core) * chips, chips)]
        return pltpu.make_async_remote_copy(
            src_ref=part, dst_ref=part, send_sem=core_send.at[c], recv_sem=core_recv.at[c],
            device_id=(chip * 2 + 1 - core, z), device_id_type=MESH,
        )

    kv_cols = 2 * k_cols

    def export_start(c):
        all_slots(recv, c, slot_recv)

        def keep(i, carry):
            for n in range(4):
                near[i * 4 + n] = recv[c, i * 4 + n]
            return carry

        lax.fori_loop(0, leafs // 4, keep, 0)
        exported = [
            near[jnp.clip(table_sm[0, 2 * ANC + 1 + k], 0, leafs - 1)].astype(jnp.float32)[:SUB]
            for k in range(EXPORT)
        ]
        far[c, place] = jnp.concatenate(exported, axis=0).astype(jnp.bfloat16)
        for step in CHIP_STEPS:
            chip_copy(step, c).start()

    def join(even, odd, k):
        at = slice(k * SUB, (k + 1) * SUB)
        return jnp.concatenate([even[at], odd[at]], axis=0).astype(jnp.bfloat16)

    def gather_near(c):
        def keep(i, carry):
            for n in range(2):
                s = i * 2 + n
                even, odd = recv[2 * c, s].astype(jnp.float32), recv[2 * c + 1, s].astype(jnp.float32)
                pool[c, s] = join(even, odd, 0)
                query[c, s] = join(even, odd, 1)
            return carry

        lax.fori_loop(0, leafs // 2, keep, 0)

    def gather_far(c):
        def keep(i, carry):
            for n in range(2):
                s = i * 2 + n
                even, odd = far[2 * c, s].astype(jnp.float32), far[2 * c + 1, s].astype(jnp.float32)
                for k in range(EXPORT):
                    pool[c, leafs + s * EXPORT + k] = join(even, odd, k)
            return carry

        lax.fori_loop(0, leafs // 2, keep, 0)

    def export_core(c):
        chips_arrived(c)
        core_copy(c).start()

    def export_end(c):
        core_arrival(2 * c).wait_recv()
        core_arrival(2 * c + 1).wait_recv()
        gather_far(c)

    heads = k_cols // HD
    groups = q_cols // k_cols
    q_rows = groups * TOK
    lane = lax.broadcasted_iota(jnp.int32, (1, ANC * TOK), 1)

    tri = lax.broadcasted_iota(jnp.int32, (q_rows, ANC * TOK), 1) <= lax.rem(
        lax.broadcasted_iota(jnp.int32, (q_rows, ANC * TOK), 0), TOK
    )
    tri = tri | (lax.broadcasted_iota(jnp.int32, (q_rows, ANC * TOK), 1) >= TOK)

    def load_queries(own, h, first, last):
        return jnp.concatenate(
            [
                query[c, own, :, pl.ds((h * groups + g) * HD, HD)]
                for c in range(first, last)
                for g in range(groups)
            ],
            axis=0,
        )

    def load_pool(places, column, first, last):
        return jnp.concatenate(
            [pool[c, p, :, pl.ds(column, HD)] for c in range(first, last) for p in places], axis=0
        )

    def attend(q0, q1, k0, k1, final):
        at = pl.ds(q0 * q_rows, (q1 - q0) * q_rows)

        def batch(slots):
            chains = [(n, h) for n in range(len(slots)) for h in range(heads)]
            places = [[place_sm[r * ANC + p] for p in range(ANC)] for r in slots]
            limit = [lane < (table_sm[r, ANC - 1] + 1) * TOK for r in slots]
            past = [x & (lane >= TOK) for x in limit]
            scores = {
                (n, h): lax.dot_general(
                    load_queries(places[n][0], h, q0, q1),
                    load_pool(places[n], h * HD, k0, k1),
                    (((1,), (1,)), ((), ())),
                    preferred_element_type=jnp.float32,
                )
                for n, h in chains
            }
            probs, sums = {}, {}
            for n, h in chains:
                capped = jnp.tanh(scores[n, h] * (query_scale / soft_cap))
                raised = jnp.exp2(capped * (soft_cap * math.log2(math.e)))
                lines, adds = [], []
                for q in range(q0, q1):
                    tiles = []
                    for k in range(k0, k1):
                        tile = raised[
                            (q - q0) * q_rows : (q - q0 + 1) * q_rows,
                            (k - k0) * ANC * TOK : (k - k0 + 1) * ANC * TOK,
                        ]
                        keep = limit[n] if k < q else past[n] if k > q else limit[n] & tri
                        tiles.append(jnp.where(keep, tile, 0.0))
                    lines.append(jnp.concatenate(tiles, axis=1))
                    adds.append(functools.reduce(lambda x, y: x + y, tiles))
                probs[n, h] = jnp.concatenate(lines, axis=0).astype(jnp.bfloat16)
                sums[n, h] = jnp.concatenate(adds, axis=0)
            parts = {
                (n, h): jnp.dot(
                    probs[n, h],
                    load_pool(places[n], k_cols + h * HD, k0, k1),
                    preferred_element_type=jnp.float32,
                )
                for n, h in chains
            }
            if not final:
                for n, h in chains:
                    numer[slots[n], h, at, :] = parts[n, h]
                    total[slots[n], h, at, :] = sums[n, h]
                return
            results = {}
            for n, h in chains:
                whole = jnp.sum(total[slots[n], h] + sums[n, h], axis=1, keepdims=True)
                result = (numer[slots[n], h] + parts[n, h]) * (1.0 / whole)
                results[n, h] = jnp.where(slots[n] < my_count, result, 0.0).astype(jnp.bfloat16)
            for n, h in chains:
                for q in range(CHUNKS):
                    for g in range(groups):
                        start = (q * groups + g) * TOK
                        out_ref[slots[n], pl.ds(q * TOK, TOK), pl.ds((h * groups + g) * HD, HD)] = results[n, h][
                            start : start + TOK
                        ]

        whole, rest = SLOTS // BATCH, SLOTS % BATCH

        def step(i, carry):
            batch([i * BATCH + n for n in range(BATCH)])
            return carry

        lax.fori_loop(0, whole, step, 0)
        if rest:
            batch(list(range(whole * BATCH, SLOTS)))

    def one_chunk(c, carry):
        accumulate(z, c, True)
        accumulate(left, c, False)
        accumulate(right, c, False)

        for k in range(CHUNKS - 2):

            @pl.when(c == 2 * k + 4)
            def _(k=k):
                gather_near(k)
                export_end(k)

        forward_arrival(0, c).wait_recv()
        forward_arrival(1, c).wait_recv()
        accumulate(opposite, c, False)

        scale = lax.rsqrt(squares[...] / width + norm_epsilon)
        cosine = angle_cos[c]
        sine = angle_sin[c]

        acc[...] += jnp.dot(scaled[...], weights[opposite], preferred_element_type=jnp.float32)

        def head(column):
            value = acc[:, pl.ds(column, HD)] * scale
            if column < q_cols + k_cols:
                value = value * cosine + pltpu.roll(value, HD // 2, 1) * sine
            return value.reshape(nodes, SUB, HD)

        for column in range(0, q_cols, HD):
            both = jnp.concatenate([head(q_cols + column), head(column)], axis=1)
            made[:, :, pl.ds(column, HD)] = both.astype(jnp.bfloat16)

        def fill(i, carry2):
            for n in range(4):
                d = i * 4 + n
                send[c, d] = made[index_sm[d]]
            return carry2

        lax.fori_loop(0, leafs // 4, fill, 0)
        for step in SLOT_STEPS:
            slot_copy(step, c).start()
        recv[c, me] = send[c, me]

        @pl.when(c >= 1)
        def _():
            export_start(c - 1)

        @pl.when(c >= 2)
        def _():
            export_core(c - 2)

        @pl.when(c + 1 < SUBS)
        def _():
            pass_on(c + 1)

        return carry

    lax.fori_loop(0, SUBS, one_chunk, 0)

    last = CHUNKS - 1
    gather_near(last - 1)
    export_end(last - 1)
    attend(0, last, 0, last, False)
    export_start(SUBS - 1)
    export_core(SUBS - 2)
    gather_near(last)
    attend(last, CHUNKS, 0, last, False)
    export_core(SUBS - 1)
    export_end(last)
    attend(0, CHUNKS, last, CHUNKS, True)

    def settle(c, carry):
        for side in (0, 1):
            full(side, 0, c).wait_send()
            full(side, 1, c).wait_send()
            forward(side, c).wait_send()
        all_slots(send, c, slot_send)
        exported = far.at[c, pl.ds(0, chips - 1)]
        pltpu.make_async_copy(exported, exported, chip_send.at[c]).wait()
        core_copy(c).wait_send()
        return carry

    lax.fori_loop(0, SUBS, settle, 0)
    pltpu.make_async_copy(ids_out.at[pl.ds(0, leafs - 1)], ids_out.at[pl.ds(0, leafs - 1)], ids_send).wait()


def hand_over(from_ref, to_ref, held, in_sems, out_sems):
    size = -(-SLOTS // OUT_PARTS)
    spans = [pl.ds(i * size, min(size, SLOTS - i * size)) for i in range(OUT_PARTS)]
    loads = [pltpu.make_async_copy(from_ref.at[at], held.at[at], in_sems.at[i]) for i, at in enumerate(spans)]
    stores = [pltpu.make_async_copy(held.at[at], to_ref.at[at], out_sems.at[i]) for i, at in enumerate(spans)]
    for load in loads:
        load.start()
    for load, store in zip(loads, stores):
        load.wait()
        store.start()
    for store in stores:
        store.wait()


def on_device(tokens, norm_gain, w_query, w_key, w_value, gen_node, partition, parent, block_mask):
    leafs = lax.axis_size("leaf")
    nodes = gen_node.shape[0]
    feat = tokens.shape[1]
    width = norm_gain.shape[0]
    q_cols = w_query.shape[1]
    k_cols = w_key.shape[1]
    cols = q_cols + 2 * k_cols
    heads = k_cols // HD
    rows = nodes * SUB
    head_rows = q_cols // k_cols * NODE_TOK
    node_total = parent.shape[0]
    half_dim = HD // 2
    inverse_freq = np.exp(
        np.arange(half_dim, dtype=np.float32) * np.float32(-2.0 * math.log(rope_base) / HD)
    ).astype(np.float32)
    freq = jnp.asarray(np.concatenate([inverse_freq, inverse_freq])[None, :])
    bf16, f32, i32 = jnp.bfloat16, jnp.float32, jnp.int32
    dma = pltpu.SemaphoreType.DMA
    smem = pl.BlockSpec(memory_space=pltpu.SMEM)
    vmem = pl.BlockSpec(memory_space=pltpu.VMEM)
    hbm = pl.BlockSpec(memory_space=pl.ANY)
    out = pl.pallas_call(
        functools.partial(fused_kernel, leafs, nodes, width, q_cols, k_cols),
        out_shape=jax.ShapeDtypeStruct((SLOTS, NODE_TOK, q_cols), bf16),
        in_specs=[smem, smem, smem, vmem, vmem, vmem, hbm, hbm, hbm, hbm],
        out_specs=vmem,
        scratch_shapes=[
            pltpu.VMEM((nodes, NODE_TOK, feat), bf16),
            pltpu.VMEM((4, SUBS, nodes // 2, TOK, feat), bf16),
            pltpu.VMEM((4, feat, cols), bf16),
            pltpu.VMEM((rows, feat), bf16),
            pltpu.VMEM((rows, cols), f32),
            pltpu.VMEM((rows, 128), f32),
            pltpu.VMEM((SUBS, rows, HD), f32),
            pltpu.VMEM((SUBS, rows, HD), f32),
            pltpu.VMEM((nodes, TOK, q_cols), bf16),
            pltpu.VMEM((SUBS, leafs, TOK, q_cols), bf16),
            pltpu.VMEM((SUBS, leafs, TOK, q_cols), bf16),
            pltpu.VMEM((leafs, TOK, q_cols), bf16),
            pltpu.VMEM((SUBS, leafs, TOK, 2 * k_cols), bf16),
            pltpu.VMEM((CHUNKS, leafs, TOK, q_cols), bf16),
            pltpu.VMEM((CHUNKS, leafs + leafs * EXPORT, TOK, 2 * k_cols), bf16),
            pltpu.VMEM((SLOTS, heads, head_rows, HD), f32),
            pltpu.VMEM((SLOTS, heads, head_rows, HD), f32),
            pltpu.VMEM((leafs, 8, 128), i32),
            pltpu.VMEM((leafs, 8, 128), i32),
            pltpu.VMEM((32, 128), i32),
            pltpu.VMEM((4, 1, feat), f32),
            pltpu.SMEM((node_total,), i32),
            pltpu.SMEM((leafs,), i32),
            pltpu.SMEM((leafs,), i32),
            pltpu.SMEM((leafs,), i32),
            pltpu.SMEM((32, 128), i32),
            pltpu.SMEM((SLOTS * ANC,), i32),
            dma((3,)),
            dma((CHUNKS,)),
            dma((2, 2, SUBS)),
            dma((2, 2, SUBS)),
            dma((2, SUBS)),
            dma((2, SUBS)),
            dma,
            dma,
            dma,
            dma((SUBS,)),
            dma((SUBS,)),
            dma((SUBS,)),
            dma((SUBS,)),
            dma((SUBS,)),
            dma((SUBS,)),
        ],
        compiler_params=pltpu.CompilerParams(
            collective_id=0, has_side_effects=True, vmem_limit_bytes=62 * 1024 * 1024
        ),
        cost_estimate=pl.CostEstimate(
            flops=2 * nodes * NODE_TOK * width * cols, bytes_accessed=30_000_000, transcendentals=0
        ),
        name="tree_attention",
    )(
        gen_node, partition, parent, block_mask, norm_gain, freq,
        tokens.reshape(nodes, NODE_TOK, feat),
        w_query.reshape(4, feat, q_cols), w_key.reshape(4, feat, k_cols), w_value.reshape(4, feat, k_cols),
    )
    return pl.pallas_call(
        hand_over,
        out_shape=jax.ShapeDtypeStruct((SLOTS, NODE_TOK, q_cols), bf16),
        in_specs=[hbm],
        out_specs=hbm,
        scratch_shapes=[pltpu.VMEM((SLOTS, NODE_TOK, q_cols), bf16), dma((OUT_PARTS,)), dma((OUT_PARTS,))],
        name="hand_over",
    )(out).reshape(CAP * NODE_TOK, q_cols)


def solution(mesh):
    in_specs = (
        P("leaf", "mp"),
        P(),
        P(None, "mp"),
        P(None, "mp"),
        P(None, "mp"),
        P("leaf"),
        P(),
        P(),
        P(),
    )
    out_specs = P("leaf", "mp")
    return jax.shard_map(
        on_device, mesh=mesh, in_specs=in_specs, out_specs=out_specs, check_vma=False
    )
```

```python
import functools
import math

import jax
import jax.numpy as jnp
import numpy as np
from jax import lax
from jax.experimental import pallas as pl
from jax.experimental.pallas import tpu as pltpu
from jax.sharding import PartitionSpec as P

HD = 128
CAP = 31
ANC = 8
EXPORT = 2
CHUNKS = 4
NODE_TOK = 64
TOK = NODE_TOK // CHUNKS
SUBS = 2 * CHUNKS
SUB = TOK // 2
SLOTS = CAP
BATCH = 8
OUT_PARTS = 8
CHIP_STEPS = [(2, 2), (0, 1), (1, 0), (0, 3), (3, 0), (2, 1), (1, 2), (2, 3), (3, 2), (0, 2), (2, 0), (1, 1), (3, 3), (1, 3), (3, 1)]
SLOT_STEPS = [(2, 2, 0), (0, 1, 0), (1, 0, 0), (0, 3, 0), (3, 0, 0), (2, 1, 0), (1, 2, 0), (2, 3, 0), (3, 2, 0), (0, 2, 0), (2, 0, 0), (1, 1, 0), (3, 3, 0), (1, 3, 0), (3, 1, 0), (2, 2, 1), (0, 1, 1), (1, 0, 1), (0, 3, 1), (3, 0, 1), (2, 1, 1), (1, 2, 1), (2, 3, 1), (3, 2, 1), (0, 2, 1), (2, 0, 1), (1, 1, 1), (3, 3, 1), (1, 3, 1), (3, 1, 1), (0, 0, 1)]

norm_epsilon = 1e-06
soft_cap = 50.0
query_scale = 144.0 ** (-0.5)
rope_base = 10000.0

MESH = pl.DeviceIdType.MESH


def fused_kernel(
    leafs, nodes, width, q_cols, k_cols,
    gen_ref, part_ref, parent_ref, mask_ref, gain_ref, freq_ref, tok_ref, wq_ref, wk_ref, wv_ref,
    out_ref,
    held, pieces, weights, scaled, acc, squares, angle_cos, angle_sin, made, send, recv, near, far,
    result_vm, query, pool, numer, total, ids_out, ids_in, table_vm, gain_vm,
    depth_sm, index_sm, start_sm, end_sm, table_sm, place_sm,
    out_sem, load_sem, own_sem, full_send, full_recv, half_send, half_recv, ids_send, ids_recv, table_sem,
    slot_send, slot_recv, chip_send, chip_recv, core_send, core_recv,
):
    me = lax.axis_index("leaf")
    z = lax.axis_index("mp")
    mp = 4
    right, left = lax.rem(z + 1, mp), lax.rem(z + 3, mp)
    opposite = lax.rem(z + 2, mp)
    feat = width // mp
    rows = nodes * SUB
    cols = q_cols + 2 * k_cols
    half = nodes // 4
    node_total = parent_ref.shape[0]
    core = lax.rem(me, 2)
    chip = lax.div(me, 2)
    chips = leafs // 2

    def chip_at(dy, dx):
        return lax.rem(lax.div(chip, 4) + dy, chips // 4) * 4 + lax.rem(lax.rem(chip, 4) + dx, 4)


    loads = [
        pltpu.make_async_copy(wq_ref, weights.at[:, :, pl.ds(0, q_cols)], load_sem.at[0]),
        pltpu.make_async_copy(wk_ref, weights.at[:, :, pl.ds(q_cols, k_cols)], load_sem.at[1]),
        pltpu.make_async_copy(wv_ref, weights.at[:, :, pl.ds(q_cols + k_cols, k_cols)], load_sem.at[2]),
    ]

    def own_load(c):
        at = pl.ds(pl.multiple_of(c * TOK, TOK), TOK)
        return pltpu.make_async_copy(tok_ref.at[:, at, :], held.at[:, at, :], own_sem.at[c])

    def deal(c):
        at = pl.ds(pl.multiple_of(c * TOK, TOK), TOK)

        def pair(j, carry):
            one = held[2 * j, at, :].astype(jnp.float32)
            two = held[2 * j + 1, at, :].astype(jnp.float32)
            pieces[z, 2 * c, j] = jnp.concatenate([one[:SUB], two[:SUB]], axis=0).astype(jnp.bfloat16)
            pieces[z, 2 * c + 1, j] = jnp.concatenate([one[SUB:], two[SUB:]], axis=0).astype(jnp.bfloat16)
            return carry

        lax.fori_loop(0, nodes // 2, pair, 0)

    barrier = pltpu.get_barrier_semaphore()

    def greet(o, carry):
        peer = lax.rem(me + o, leafs)
        pl.semaphore_signal(barrier, inc=1, device_id=(peer, z), device_id_type=MESH)
        return carry

    lax.fori_loop(1, leafs, greet, 0)
    pl.semaphore_signal(barrier, inc=1, device_id=(me, right), device_id_type=MESH)
    pl.semaphore_signal(barrier, inc=1, device_id=(me, left), device_id_type=MESH)
    for c in range(CHUNKS):
        own_load(c).start()
    for load in loads:
        load.start()
    pl.semaphore_wait(barrier, leafs + 1)

    def full(side, part, c):
        piece = pieces.at[z, c, pl.ds(part * half, half)]
        return pltpu.make_async_remote_copy(
            src_ref=piece,
            dst_ref=piece,
            send_sem=full_send.at[side, part, c],
            recv_sem=full_recv.at[side, part, c],
            device_id=(me, right if side == 0 else left),
            device_id_type=MESH,
        )

    def full_arrival(side, part, c):
        piece = pieces.at[left if side == 0 else right, c, pl.ds(part * half, half)]
        return pltpu.make_async_remote_copy(
            src_ref=piece,
            dst_ref=piece,
            send_sem=full_send.at[side, part, c],
            recv_sem=full_recv.at[side, part, c],
            device_id=(me, right if side == 0 else left),
            device_id_type=MESH,
        )

    def forward(side, c):
        source = left if side == 0 else right
        part = pieces.at[source, c, pl.ds(side * half, half)]
        return pltpu.make_async_remote_copy(
            src_ref=part,
            dst_ref=part,
            send_sem=half_send.at[side, c],
            recv_sem=half_recv.at[side, c],
            device_id=(me, right if side == 0 else left),
            device_id_type=MESH,
        )

    def forward_arrival(side, c):
        part = pieces.at[opposite, c, pl.ds(side * half, half)]
        return pltpu.make_async_remote_copy(
            src_ref=part,
            dst_ref=part,
            send_sem=half_send.at[side, c],
            recv_sem=half_recv.at[side, c],
            device_id=(me, right if side == 0 else left),
            device_id_type=MESH,
        )

    for c in range(CHUNKS):
        own_load(c).wait()
    for c in range(CHUNKS):
        deal(c)
        if c == 0:
            for step in (0, 1):
                for side in (0, 1):
                    full(side, side ^ step, 0).start()

    def pass_on(c, between=None):
        for side in (0, 1):
            full_arrival(side, side, c).wait_recv()
            forward(side, c).start()

        @pl.when(c + 1 < SUBS)
        def _():
            for side in (0, 1):
                full(side, side, c + 1).start()

        if between is not None:
            between()
        for side in (0, 1):
            full_arrival(side, 1 - side, c).wait_recv()

        @pl.when(c + 1 < SUBS)
        def _():
            for side in (0, 1):
                full(side, 1 - side, c + 1).start()

    for part in range(mp):
        gain_vm[part] = gain_ref[pl.ds(part * feat, feat)].astype(jnp.float32).reshape(1, feat)

    def ranges(d, first):
        last = first + part_ref[d]
        start_sm[d] = first
        end_sm[d] = last
        found = jnp.int32(0)
        for b in range(nodes):
            node = gen_ref[b]
            found = found + jnp.where((node >= first) & (node < last), b + 1, 0)
        local = jnp.clip(found - 1, 0, nodes - 1)
        index_sm[d] = local
        ids_out[d] = jnp.full((8, 128), jnp.where(found > 0, gen_ref[local], -1), jnp.int32)
        return last

    lax.fori_loop(0, leafs, ranges, jnp.int32(0))

    def ids_copy(o):
        peer = lax.rem(me + o, leafs)
        return pltpu.make_async_remote_copy(
            src_ref=ids_out.at[peer],
            dst_ref=ids_in.at[me],
            send_sem=ids_send,
            recv_sem=ids_recv,
            device_id=(peer, z),
            device_id_type=MESH,
        )

    lax.fori_loop(1, leafs, lambda o, carry: (ids_copy(o).start(), carry)[1], 0)
    ids_in[me] = ids_out[me]

    depth_sm[0] = jnp.int32(0)

    def deeper(n, carry):
        depth_sm[n] = depth_sm[parent_ref[n]] + 1
        return carry

    lax.fori_loop(1, node_total, deeper, 0)

    pass_on(jnp.int32(0))

    token_row = lax.broadcasted_iota(jnp.int32, (SUB, HD), 0)
    sign = jnp.where(lax.broadcasted_iota(jnp.int32, (rows, HD), 1) < HD // 2, -1.0, 1.0)

    def tables(c, carry):
        def one_node(b, carry2):
            position = depth_sm[gen_ref[b]] * NODE_TOK + c * SUB + token_row
            at = pl.ds(pl.multiple_of(b * SUB, SUB), SUB)
            angle_cos[c, at, :] = position.astype(jnp.float32) * freq_ref[...]
            return carry2

        lax.fori_loop(0, nodes, one_node, 0)
        angles = angle_cos[c]
        angle_sin[c] = jnp.sin(angles) * sign
        angle_cos[c] = jnp.cos(angles)
        return carry

    lax.fori_loop(0, SUBS, tables, 0)

    lane8 = lax.broadcasted_iota(jnp.int32, (8, node_total), 1)

    def spans(step, carry):
        d = leafs - 1 - step
        end_of, start_of, owner = carry
        inside = lane8 < end_sm[d]
        return (
            jnp.where(inside, end_sm[d], end_of),
            jnp.where(inside, start_sm[d], start_of),
            jnp.where(inside, d, owner),
        )

    blank = jnp.zeros((8, node_total), jnp.int32)
    end_of, start_of, owner = lax.fori_loop(0, leafs, spans, (blank, blank, blank))
    my_start = start_sm[me]
    row_id = lax.broadcasted_iota(jnp.int32, (node_total, node_total), 0)
    col_id = lax.broadcasted_iota(jnp.int32, (node_total, node_total), 1)
    mask = mask_ref[...]
    foreign = (mask > 0) & (row_id >= end_of[0:1, :])
    seen = jnp.max(jnp.where(foreign, 1.0, 0.0), axis=0, keepdims=True)
    earlier = jnp.where((row_id < col_id) & (row_id >= start_of[0:1, :]), 1.0, 0.0).astype(jnp.bfloat16)
    seen8 = jnp.broadcast_to(seen, (8, node_total))
    rank8 = jnp.dot(seen8.astype(jnp.bfloat16), earlier, preferred_element_type=jnp.float32)
    owner_f = owner.astype(jnp.float32)
    core_f = lax.rem(owner, 2).astype(jnp.float32)
    chip_f = lax.div(owner, 2).astype(jnp.float32)
    far_place = leafs + core_f * leafs + chip_f * EXPORT + jnp.minimum(rank8, EXPORT - 1.0)
    relative = (lane8 - my_start).astype(jnp.float32)
    place = jnp.where(lane8 >= my_start, relative, far_place)

    slot_row = lax.broadcasted_iota(jnp.int32, (32, node_total), 0)
    slot_col = lax.broadcasted_iota(jnp.int32, (32, node_total), 1)
    own_here = slot_col == my_start + slot_row
    own_mask = jnp.dot(
        jnp.where(own_here, 1.0, 0.0).astype(jnp.bfloat16),
        jnp.where(mask > 0, 1.0, 0.0).astype(jnp.bfloat16),
        preferred_element_type=jnp.float32,
    )
    others = jnp.where((own_mask > 0.5) & ~own_here, 1.0, 0.0)
    before = jnp.where(row_id < col_id, 1.0, 0.0).astype(jnp.bfloat16)
    rank = jnp.dot(others.astype(jnp.bfloat16), before, preferred_element_type=jnp.float32)
    lane32 = lax.broadcasted_iota(jnp.int32, (32, 128), 1)
    row32 = lax.broadcasted_iota(jnp.int32, (32, 128), 0)
    table = jnp.zeros((32, 128), jnp.float32)
    for r in range(ANC - 1):
        hit = (others > 0.5) & (jnp.abs(rank - float(r)) < 0.5)
        value = jnp.sum(jnp.where(hit, place[0:1, :], 0.0), axis=1, keepdims=True)
        table = jnp.where(lane32 == r, value, table)
    table = jnp.where(lane32 == ANC - 1, jnp.sum(others, axis=1, keepdims=True), table)

    pltpu.make_async_copy(ids_in.at[pl.ds(0, leafs - 1)], ids_in.at[pl.ds(0, leafs - 1)], ids_recv).wait()

    def sources(s, total):
        return total + jnp.where(ids_in[s][0:1, :] == my_start + row32, s.astype(jnp.float32), 0.0)

    source = lax.fori_loop(0, leafs, sources, jnp.zeros((32, 128), jnp.float32))
    table = jnp.where(lane32 == 2 * ANC, source, table)
    mine8 = (lane8 >= my_start) & (owner == me) & (seen8 > 0.5)
    for k in range(EXPORT):
        picked = jnp.sum(
            jnp.where(mine8 & (jnp.abs(rank8 - float(k)) < 0.5), relative, 0.0), axis=1, keepdims=True
        )
        chosen = jnp.sum(
            jnp.where(row32.astype(jnp.float32) == picked[0:1, :], source, 0.0), axis=0, keepdims=True
        )
        table = jnp.where(lane32 == 2 * ANC + 1 + k, chosen, table)
    table_vm[...] = table.astype(jnp.int32)
    to_scalars = pltpu.make_async_copy(table_vm, table_sm, table_sem)
    to_scalars.start()
    to_scalars.wait()

    def find_places(r, carry):
        place_sm[r * ANC] = jnp.clip(table_sm[r, 2 * ANC], 0, leafs - 1)
        for p in range(ANC - 1):
            v = table_sm[r, p]
            near = table_sm[jnp.clip(v, 0, leafs - 1), 2 * ANC]
            place_sm[r * ANC + p + 1] = jnp.clip(jnp.where(v < leafs, near, v), 0, leafs + leafs * EXPORT - 1)
        return carry

    lax.fori_loop(0, SLOTS, find_places, 0)
    my_count = part_ref[me]

    for load in loads:
        load.wait()
    def accumulate(src, c, first):
        wide = pieces[src, c].reshape(rows, feat).astype(jnp.float32)
        gain = gain_vm[src]
        scaled[...] = (wide * gain).astype(jnp.bfloat16)
        part = jnp.sum(wide * wide, axis=1, keepdims=True)
        if first:
            squares[...] = jnp.broadcast_to(part, (rows, 128))
        else:
            squares[...] += jnp.broadcast_to(part, (rows, 128))
        if src is opposite:
            return
        product = jnp.dot(scaled[...], weights[src], preferred_element_type=jnp.float32)
        if first:
            acc[...] = product
        else:
            acc[...] += product

    def slot_copy(step, c):
        peer = chip_at(step[0], step[1]) * 2 + lax.rem(core + step[2], 2)
        return pltpu.make_async_remote_copy(
            src_ref=send.at[c, peer],
            dst_ref=recv.at[c, me],
            send_sem=slot_send.at[c],
            recv_sem=slot_recv.at[c],
            device_id=(peer, z),
            device_id_type=MESH,
        )

    def all_slots(buffer, c, sem):
        part = buffer.at[c, pl.ds(0, leafs - 1)]
        pltpu.make_async_copy(part, part, sem.at[c]).wait()

    place = core * chips + chip

    def chip_copy(step, c):
        part = far.at[c, place]
        return pltpu.make_async_remote_copy(
            src_ref=part, dst_ref=part, send_sem=chip_send.at[c], recv_sem=chip_recv.at[c],
            device_id=(chip_at(step[0], step[1]) * 2 + core, z), device_id_type=MESH,
        )

    def chips_arrived(c):
        part = far.at[c, pl.ds(0, chips - 1)]
        pltpu.make_async_copy(part, part, chip_recv.at[c]).wait()

    def core_copy(c):
        part = far.at[c, pl.ds(core * chips, chips)]
        return pltpu.make_async_remote_copy(
            src_ref=part, dst_ref=part, send_sem=core_send.at[c], recv_sem=core_recv.at[c],
            device_id=(chip * 2 + 1 - core, z), device_id_type=MESH,
        )

    def core_arrival(c):
        part = far.at[c, pl.ds((1 - core) * chips, chips)]
        return pltpu.make_async_remote_copy(
            src_ref=part, dst_ref=part, send_sem=core_send.at[c], recv_sem=core_recv.at[c],
            device_id=(chip * 2 + 1 - core, z), device_id_type=MESH,
        )

    kv_cols = 2 * k_cols

    def export_start(c):
        all_slots(recv, c, slot_recv)

        def keep(i, carry):
            for n in range(4):
                near[i * 4 + n] = recv[c, i * 4 + n]
            return carry

        lax.fori_loop(0, leafs // 4, keep, 0)
        exported = [
            near[jnp.clip(table_sm[0, 2 * ANC + 1 + k], 0, leafs - 1)].astype(jnp.float32)[:SUB]
            for k in range(EXPORT)
        ]
        far[c, place] = jnp.concatenate(exported, axis=0).astype(jnp.bfloat16)
        for step in CHIP_STEPS:
            chip_copy(step, c).start()

    def join(even, odd, k):
        at = slice(k * SUB, (k + 1) * SUB)
        return jnp.concatenate([even[at], odd[at]], axis=0).astype(jnp.bfloat16)

    def gather_near(c):
        def keep(i, carry):
            for n in range(2):
                s = i * 2 + n
                even, odd = recv[2 * c, s].astype(jnp.float32), recv[2 * c + 1, s].astype(jnp.float32)
                pool[c, s] = join(even, odd, 0)
                query[c, s] = join(even, odd, 1)
            return carry

        lax.fori_loop(0, leafs // 2, keep, 0)

    def gather_far(c):
        def keep(i, carry):
            for n in range(2):
                s = i * 2 + n
                even, odd = far[2 * c, s].astype(jnp.float32), far[2 * c + 1, s].astype(jnp.float32)
                for k in range(EXPORT):
                    pool[c, leafs + s * EXPORT + k] = join(even, odd, k)
            return carry

        lax.fori_loop(0, leafs // 2, keep, 0)

    def export_core(c):
        chips_arrived(c)
        core_copy(c).start()

    def export_end(c):
        core_arrival(2 * c).wait_recv()
        core_arrival(2 * c + 1).wait_recv()
        gather_far(c)

    heads = k_cols // HD
    groups = q_cols // k_cols
    q_rows = groups * TOK
    lane = lax.broadcasted_iota(jnp.int32, (1, ANC * TOK), 1)

    tri = lax.broadcasted_iota(jnp.int32, (q_rows, ANC * TOK), 1) <= lax.rem(
        lax.broadcasted_iota(jnp.int32, (q_rows, ANC * TOK), 0), TOK
    )
    tri = tri | (lax.broadcasted_iota(jnp.int32, (q_rows, ANC * TOK), 1) >= TOK)

    def load_queries(own, h, first, last):
        return jnp.concatenate(
            [
                query[c, own, :, pl.ds((h * groups + g) * HD, HD)]
                for c in range(first, last)
                for g in range(groups)
            ],
            axis=0,
        )

    def load_pool(places, column, first, last):
        return jnp.concatenate(
            [pool[c, p, :, pl.ds(column, HD)] for c in range(first, last) for p in places], axis=0
        )

    def attend(q0, q1, k0, k1, final):
        at = pl.ds(q0 * q_rows, (q1 - q0) * q_rows)

        def batch(slots):
            chains = [(n, h) for n in range(len(slots)) for h in range(heads)]
            places = [[place_sm[r * ANC + p] for p in range(ANC)] for r in slots]
            limit = [lane < (table_sm[r, ANC - 1] + 1) * TOK for r in slots]
            past = [x & (lane >= TOK) for x in limit]
            scores = {
                (n, h): lax.dot_general(
                    load_queries(places[n][0], h, q0, q1),
                    load_pool(places[n], h * HD, k0, k1),
                    (((1,), (1,)), ((), ())),
                    preferred_element_type=jnp.float32,
                )
                for n, h in chains
            }
            probs, sums = {}, {}
            for n, h in chains:
                capped = jnp.tanh(scores[n, h] * (query_scale / soft_cap))
                raised = jnp.exp2(capped * (soft_cap * math.log2(math.e)))
                lines, adds = [], []
                for q in range(q0, q1):
                    tiles = []
                    for k in range(k0, k1):
                        tile = raised[
                            (q - q0) * q_rows : (q - q0 + 1) * q_rows,
                            (k - k0) * ANC * TOK : (k - k0 + 1) * ANC * TOK,
                        ]
                        keep = limit[n] if k < q else past[n] if k > q else limit[n] & tri
                        tiles.append(jnp.where(keep, tile, 0.0))
                    lines.append(jnp.concatenate(tiles, axis=1))
                    adds.append(functools.reduce(lambda x, y: x + y, tiles))
                probs[n, h] = jnp.concatenate(lines, axis=0).astype(jnp.bfloat16)
                sums[n, h] = jnp.concatenate(adds, axis=0)
            parts = {
                (n, h): jnp.dot(
                    probs[n, h],
                    load_pool(places[n], k_cols + h * HD, k0, k1),
                    preferred_element_type=jnp.float32,
                )
                for n, h in chains
            }
            if not final:
                for n, h in chains:
                    numer[slots[n], h, at, :] = parts[n, h]
                    total[slots[n], h, at, :] = sums[n, h]
                return
            results = {}
            for n, h in chains:
                whole = jnp.sum(total[slots[n], h] + sums[n, h], axis=1, keepdims=True)
                result = (numer[slots[n], h] + parts[n, h]) * (1.0 / whole)
                results[n, h] = jnp.where(slots[n] < my_count, result, 0.0).astype(jnp.bfloat16)
            for n, h in chains:
                for q in range(CHUNKS):
                    for g in range(groups):
                        start = (q * groups + g) * TOK
                        result_vm[slots[n], pl.ds(q * TOK, TOK), pl.ds((h * groups + g) * HD, HD)] = results[n, h][
                            start : start + TOK
                        ]

        def store(i, size):
            at = pl.ds(i * BATCH, size)
            return pltpu.make_async_copy(result_vm.at[at], out_ref.at[at], out_sem.at[i])

        whole, rest = SLOTS // BATCH, SLOTS % BATCH

        def step(i, carry):
            batch([i * BATCH + n for n in range(BATCH)])
            if final:
                store(i, BATCH).start()
            return carry

        lax.fori_loop(0, whole, step, 0)
        if rest:
            batch(list(range(whole * BATCH, SLOTS)))
        if final:
            if rest:
                store(whole, rest).start()
                store(whole, rest).wait()
            for i in range(whole):
                store(i, BATCH).wait()

    def one_chunk(c, carry):
        accumulate(z, c, True)
        accumulate(left, c, False)
        accumulate(right, c, False)

        for k in range(CHUNKS - 2):

            @pl.when(c == 2 * k + 4)
            def _(k=k):
                gather_near(k)
                export_end(k)

        forward_arrival(0, c).wait_recv()
        forward_arrival(1, c).wait_recv()
        accumulate(opposite, c, False)

        scale = lax.rsqrt(squares[...] / width + norm_epsilon)
        cosine = angle_cos[c]
        sine = angle_sin[c]

        acc[...] += jnp.dot(scaled[...], weights[opposite], preferred_element_type=jnp.float32)

        def head(column):
            value = acc[:, pl.ds(column, HD)] * scale
            if column < q_cols + k_cols:
                value = value * cosine + pltpu.roll(value, HD // 2, 1) * sine
            return value.reshape(nodes, SUB, HD)

        for column in range(0, q_cols, HD):
            both = jnp.concatenate([head(q_cols + column), head(column)], axis=1)
            made[:, :, pl.ds(column, HD)] = both.astype(jnp.bfloat16)

        def fill(i, carry2):
            for n in range(4):
                d = i * 4 + n
                send[c, d] = made[index_sm[d]]
            return carry2

        lax.fori_loop(0, leafs // 4, fill, 0)
        for step in SLOT_STEPS:
            slot_copy(step, c).start()
        recv[c, me] = send[c, me]

        def exports():
            @pl.when(c >= 1)
            def _():
                export_start(c - 1)

            @pl.when(c >= 2)
            def _():
                export_core(c - 2)

        @pl.when(c + 1 < SUBS)
        def _():
            pass_on(c + 1, exports)

        @pl.when(c + 1 == SUBS)
        def _():
            exports()

        return carry

    lax.fori_loop(0, SUBS, one_chunk, 0)

    last = CHUNKS - 1
    gather_near(last - 1)
    export_end(last - 1)
    attend(0, last, 0, last, False)
    export_start(SUBS - 1)
    export_core(SUBS - 2)
    gather_near(last)
    attend(last, CHUNKS, 0, last, False)
    export_core(SUBS - 1)
    export_end(last)
    attend(0, CHUNKS, last, CHUNKS, True)

    def settle(c, carry):
        for side in (0, 1):
            full(side, 0, c).wait_send()
            full(side, 1, c).wait_send()
            forward(side, c).wait_send()
        all_slots(send, c, slot_send)
        exported = far.at[c, pl.ds(0, chips - 1)]
        pltpu.make_async_copy(exported, exported, chip_send.at[c]).wait()
        core_copy(c).wait_send()
        return carry

    lax.fori_loop(0, SUBS, settle, 0)
    pltpu.make_async_copy(ids_out.at[pl.ds(0, leafs - 1)], ids_out.at[pl.ds(0, leafs - 1)], ids_send).wait()


def hand_over(from_ref, to_ref, held, in_sems, out_sems):
    size = -(-SLOTS // OUT_PARTS)
    spans = [pl.ds(i * size, min(size, SLOTS - i * size)) for i in range(OUT_PARTS)]
    loads = [pltpu.make_async_copy(from_ref.at[at], held.at[at], in_sems.at[i]) for i, at in enumerate(spans)]
    stores = [pltpu.make_async_copy(held.at[at], to_ref.at[at], out_sems.at[i]) for i, at in enumerate(spans)]
    for load in loads:
        load.start()
    for load, store in zip(loads, stores):
        load.wait()
        store.start()
    for store in stores:
        store.wait()


def on_device(tokens, norm_gain, w_query, w_key, w_value, gen_node, partition, parent, block_mask):
    leafs = lax.axis_size("leaf")
    nodes = gen_node.shape[0]
    feat = tokens.shape[1]
    width = norm_gain.shape[0]
    q_cols = w_query.shape[1]
    k_cols = w_key.shape[1]
    cols = q_cols + 2 * k_cols
    heads = k_cols // HD
    rows = nodes * SUB
    head_rows = q_cols // k_cols * NODE_TOK
    node_total = parent.shape[0]
    half_dim = HD // 2
    inverse_freq = np.exp(
        np.arange(half_dim, dtype=np.float32) * np.float32(-2.0 * math.log(rope_base) / HD)
    ).astype(np.float32)
    freq = jnp.asarray(np.concatenate([inverse_freq, inverse_freq])[None, :])
    bf16, f32, i32 = jnp.bfloat16, jnp.float32, jnp.int32
    dma = pltpu.SemaphoreType.DMA
    smem = pl.BlockSpec(memory_space=pltpu.SMEM)
    vmem = pl.BlockSpec(memory_space=pltpu.VMEM)
    hbm = pl.BlockSpec(memory_space=pl.ANY)
    out = pl.pallas_call(
        functools.partial(fused_kernel, leafs, nodes, width, q_cols, k_cols),
        out_shape=jax.ShapeDtypeStruct((SLOTS, NODE_TOK, q_cols), bf16),
        in_specs=[smem, smem, smem, vmem, vmem, vmem, hbm, hbm, hbm, hbm],
        out_specs=hbm,
        scratch_shapes=[
            pltpu.VMEM((nodes, NODE_TOK, feat), bf16),
            pltpu.VMEM((4, SUBS, nodes // 2, TOK, feat), bf16),
            pltpu.VMEM((4, feat, cols), bf16),
            pltpu.VMEM((rows, feat), bf16),
            pltpu.VMEM((rows, cols), f32),
            pltpu.VMEM((rows, 128), f32),
            pltpu.VMEM((SUBS, rows, HD), f32),
            pltpu.VMEM((SUBS, rows, HD), f32),
            pltpu.VMEM((nodes, TOK, q_cols), bf16),
            pltpu.VMEM((SUBS, leafs, TOK, q_cols), bf16),
            pltpu.VMEM((SUBS, leafs, TOK, q_cols), bf16),
            pltpu.VMEM((leafs, TOK, q_cols), bf16),
            pltpu.VMEM((SUBS, leafs, TOK, 2 * k_cols), bf16),
            pltpu.VMEM((SLOTS, NODE_TOK, q_cols), bf16),
            pltpu.VMEM((CHUNKS, leafs, TOK, q_cols), bf16),
            pltpu.VMEM((CHUNKS, leafs + leafs * EXPORT, TOK, 2 * k_cols), bf16),
            pltpu.VMEM((SLOTS, heads, head_rows, HD), f32),
            pltpu.VMEM((SLOTS, heads, head_rows, HD), f32),
            pltpu.VMEM((leafs, 8, 128), i32),
            pltpu.VMEM((leafs, 8, 128), i32),
            pltpu.VMEM((32, 128), i32),
            pltpu.VMEM((4, 1, feat), f32),
            pltpu.SMEM((node_total,), i32),
            pltpu.SMEM((leafs,), i32),
            pltpu.SMEM((leafs,), i32),
            pltpu.SMEM((leafs,), i32),
            pltpu.SMEM((32, 128), i32),
            pltpu.SMEM((SLOTS * ANC,), i32),
            dma((-(-SLOTS // BATCH),)),
            dma((3,)),
            dma((CHUNKS,)),
            dma((2, 2, SUBS)),
            dma((2, 2, SUBS)),
            dma((2, SUBS)),
            dma((2, SUBS)),
            dma,
            dma,
            dma,
            dma((SUBS,)),
            dma((SUBS,)),
            dma((SUBS,)),
            dma((SUBS,)),
            dma((SUBS,)),
            dma((SUBS,)),
        ],
        compiler_params=pltpu.CompilerParams(
            collective_id=0, has_side_effects=True, vmem_limit_bytes=62 * 1024 * 1024
        ),
        cost_estimate=pl.CostEstimate(
            flops=2 * nodes * NODE_TOK * width * cols, bytes_accessed=30_000_000, transcendentals=0
        ),
        name="tree_attention",
    )(
        gen_node, partition, parent, block_mask, norm_gain, freq,
        tokens.reshape(nodes, NODE_TOK, feat),
        w_query.reshape(4, feat, q_cols), w_key.reshape(4, feat, k_cols), w_value.reshape(4, feat, k_cols),
    )
    return pl.pallas_call(
        hand_over,
        out_shape=jax.ShapeDtypeStruct((SLOTS, NODE_TOK, q_cols), bf16),
        in_specs=[hbm],
        out_specs=hbm,
        scratch_shapes=[pltpu.VMEM((SLOTS, NODE_TOK, q_cols), bf16), dma((OUT_PARTS,)), dma((OUT_PARTS,))],
        name="hand_over",
    )(out).reshape(CAP * NODE_TOK, q_cols)


def solution(mesh):
    in_specs = (
        P("leaf", "mp"),
        P(),
        P(None, "mp"),
        P(None, "mp"),
        P(None, "mp"),
        P("leaf"),
        P(),
        P(),
        P(),
    )
    out_specs = P("leaf", "mp")
    return jax.shard_map(
        on_device, mesh=mesh, in_specs=in_specs, out_specs=out_specs, check_vma=False
    )
```

```python
import functools
import math

import jax
import jax.numpy as jnp
import numpy as np
from jax import lax
from jax.experimental import pallas as pl
from jax.experimental.pallas import tpu as pltpu
from jax.sharding import PartitionSpec as P

HD = 128
CAP = 31
ANC = 8
EXPORT = 2
CHUNKS = 4
NODE_TOK = 64
TOK = NODE_TOK // CHUNKS
SUBS = 2 * CHUNKS
SUB = TOK // 2
SLOTS = CAP
BATCH = 16
OUT_PARTS = 8
CHIP_STEPS = [(2, 2), (0, 1), (1, 0), (0, 3), (3, 0), (2, 1), (1, 2), (2, 3), (3, 2), (0, 2), (2, 0), (1, 1), (3, 3), (1, 3), (3, 1)]
SLOT_STEPS = [(2, 2, 0), (0, 1, 0), (1, 0, 0), (0, 3, 0), (3, 0, 0), (2, 1, 0), (1, 2, 0), (2, 3, 0), (3, 2, 0), (0, 2, 0), (2, 0, 0), (1, 1, 0), (3, 3, 0), (1, 3, 0), (3, 1, 0), (2, 2, 1), (0, 1, 1), (1, 0, 1), (0, 3, 1), (3, 0, 1), (2, 1, 1), (1, 2, 1), (2, 3, 1), (3, 2, 1), (0, 2, 1), (2, 0, 1), (1, 1, 1), (3, 3, 1), (1, 3, 1), (3, 1, 1), (0, 0, 1)]

norm_epsilon = 1e-06
soft_cap = 50.0
query_scale = 144.0 ** (-0.5)
rope_base = 10000.0

MESH = pl.DeviceIdType.MESH


def fused_kernel(
    leafs, nodes, width, q_cols, k_cols,
    gen_ref, part_ref, parent_ref, mask_ref, gain_ref, freq_ref, tok_ref, wq_ref, wk_ref, wv_ref,
    out_ref,
    held, pieces, weights, scaled, acc, squares, angle_cos, angle_sin, made, send, recv, near, far,
    result_vm, query, pool, numer, total, ids_out, ids_in, table_vm, gain_vm,
    depth_sm, index_sm, start_sm, end_sm, table_sm, place_sm,
    out_sem, load_sem, own_sem, full_send, full_recv, half_send, half_recv, ids_send, ids_recv, table_sem,
    slot_send, slot_recv, chip_send, chip_recv, core_send, core_recv,
):
    me = lax.axis_index("leaf")
    z = lax.axis_index("mp")
    mp = 4
    right, left = lax.rem(z + 1, mp), lax.rem(z + 3, mp)
    opposite = lax.rem(z + 2, mp)
    feat = width // mp
    rows = nodes * SUB
    cols = q_cols + 2 * k_cols
    half = nodes // 4
    node_total = parent_ref.shape[0]
    core = lax.rem(me, 2)
    chip = lax.div(me, 2)
    chips = leafs // 2

    def chip_at(dy, dx):
        return lax.rem(lax.div(chip, 4) + dy, chips // 4) * 4 + lax.rem(lax.rem(chip, 4) + dx, 4)


    loads = [
        pltpu.make_async_copy(wq_ref, weights.at[:, :, pl.ds(0, q_cols)], load_sem.at[0]),
        pltpu.make_async_copy(wk_ref, weights.at[:, :, pl.ds(q_cols, k_cols)], load_sem.at[1]),
        pltpu.make_async_copy(wv_ref, weights.at[:, :, pl.ds(q_cols + k_cols, k_cols)], load_sem.at[2]),
    ]

    def own_load(c):
        at = pl.ds(pl.multiple_of(c * TOK, TOK), TOK)
        return pltpu.make_async_copy(tok_ref.at[:, at, :], held.at[:, at, :], own_sem.at[c])

    def deal(c):
        at = pl.ds(pl.multiple_of(c * TOK, TOK), TOK)

        def pair(j, carry):
            one = held[2 * j, at, :].astype(jnp.float32)
            two = held[2 * j + 1, at, :].astype(jnp.float32)
            pieces[z, 2 * c, j] = jnp.concatenate([one[:SUB], two[:SUB]], axis=0).astype(jnp.bfloat16)
            pieces[z, 2 * c + 1, j] = jnp.concatenate([one[SUB:], two[SUB:]], axis=0).astype(jnp.bfloat16)
            return carry

        lax.fori_loop(0, nodes // 2, pair, 0)

    barrier = pltpu.get_barrier_semaphore()

    def greet(o, carry):
        peer = lax.rem(me + o, leafs)
        pl.semaphore_signal(barrier, inc=1, device_id=(peer, z), device_id_type=MESH)
        return carry

    lax.fori_loop(1, leafs, greet, 0)
    pl.semaphore_signal(barrier, inc=1, device_id=(me, right), device_id_type=MESH)
    pl.semaphore_signal(barrier, inc=1, device_id=(me, left), device_id_type=MESH)
    for c in range(CHUNKS):
        own_load(c).start()
    for load in loads:
        load.start()
    pl.semaphore_wait(barrier, leafs + 1)

    def full(side, part, c):
        piece = pieces.at[z, c, pl.ds(part * half, half)]
        return pltpu.make_async_remote_copy(
            src_ref=piece,
            dst_ref=piece,
            send_sem=full_send.at[side, part, c],
            recv_sem=full_recv.at[side, part, c],
            device_id=(me, right if side == 0 else left),
            device_id_type=MESH,
        )

    def full_arrival(side, part, c):
        piece = pieces.at[left if side == 0 else right, c, pl.ds(part * half, half)]
        return pltpu.make_async_remote_copy(
            src_ref=piece,
            dst_ref=piece,
            send_sem=full_send.at[side, part, c],
            recv_sem=full_recv.at[side, part, c],
            device_id=(me, right if side == 0 else left),
            device_id_type=MESH,
        )

    def forward(side, c):
        source = left if side == 0 else right
        part = pieces.at[source, c, pl.ds(side * half, half)]
        return pltpu.make_async_remote_copy(
            src_ref=part,
            dst_ref=part,
            send_sem=half_send.at[side, c],
            recv_sem=half_recv.at[side, c],
            device_id=(me, right if side == 0 else left),
            device_id_type=MESH,
        )

    def forward_arrival(side, c):
        part = pieces.at[opposite, c, pl.ds(side * half, half)]
        return pltpu.make_async_remote_copy(
            src_ref=part,
            dst_ref=part,
            send_sem=half_send.at[side, c],
            recv_sem=half_recv.at[side, c],
            device_id=(me, right if side == 0 else left),
            device_id_type=MESH,
        )

    for c in range(CHUNKS):
        own_load(c).wait()
    for c in range(CHUNKS):
        deal(c)
        if c == 0:
            for step in (0, 1):
                for side in (0, 1):
                    full(side, side ^ step, 0).start()

    def pass_on(c, between=None):
        for side in (0, 1):
            full_arrival(side, side, c).wait_recv()
            forward(side, c).start()

        @pl.when(c + 1 < SUBS)
        def _():
            for side in (0, 1):
                full(side, side, c + 1).start()

        if between is not None:
            between()
        for side in (0, 1):
            full_arrival(side, 1 - side, c).wait_recv()

        @pl.when(c + 1 < SUBS)
        def _():
            for side in (0, 1):
                full(side, 1 - side, c + 1).start()

    for part in range(mp):
        gain_vm[part] = gain_ref[pl.ds(part * feat, feat)].astype(jnp.float32).reshape(1, feat)

    def ranges(d, first):
        last = first + part_ref[d]
        start_sm[d] = first
        end_sm[d] = last
        found = jnp.int32(0)
        for b in range(nodes):
            node = gen_ref[b]
            found = found + jnp.where((node >= first) & (node < last), b + 1, 0)
        local = jnp.clip(found - 1, 0, nodes - 1)
        index_sm[d] = local
        ids_out[d] = jnp.full((8, 128), jnp.where(found > 0, gen_ref[local], -1), jnp.int32)
        return last

    lax.fori_loop(0, leafs, ranges, jnp.int32(0))

    def ids_copy(o):
        peer = lax.rem(me + o, leafs)
        return pltpu.make_async_remote_copy(
            src_ref=ids_out.at[peer],
            dst_ref=ids_in.at[me],
            send_sem=ids_send,
            recv_sem=ids_recv,
            device_id=(peer, z),
            device_id_type=MESH,
        )

    lax.fori_loop(1, leafs, lambda o, carry: (ids_copy(o).start(), carry)[1], 0)
    ids_in[me] = ids_out[me]

    depth_sm[0] = jnp.int32(0)

    def deeper(n, carry):
        depth_sm[n] = depth_sm[parent_ref[n]] + 1
        return carry

    lax.fori_loop(1, node_total, deeper, 0)

    pass_on(jnp.int32(0))

    token_row = lax.broadcasted_iota(jnp.int32, (SUB, HD), 0)
    sign = jnp.where(lax.broadcasted_iota(jnp.int32, (rows, HD), 1) < HD // 2, -1.0, 1.0)

    def tables(c, carry):
        def one_node(b, carry2):
            position = depth_sm[gen_ref[b]] * NODE_TOK + c * SUB + token_row
            at = pl.ds(pl.multiple_of(b * SUB, SUB), SUB)
            angle_cos[c, at, :] = position.astype(jnp.float32) * freq_ref[...]
            return carry2

        lax.fori_loop(0, nodes, one_node, 0)
        angles = angle_cos[c]
        angle_sin[c] = jnp.sin(angles) * sign
        angle_cos[c] = jnp.cos(angles)
        return carry

    lax.fori_loop(0, SUBS, tables, 0)

    lane8 = lax.broadcasted_iota(jnp.int32, (8, node_total), 1)

    def spans(step, carry):
        d = leafs - 1 - step
        end_of, start_of, owner = carry
        inside = lane8 < end_sm[d]
        return (
            jnp.where(inside, end_sm[d], end_of),
            jnp.where(inside, start_sm[d], start_of),
            jnp.where(inside, d, owner),
        )

    blank = jnp.zeros((8, node_total), jnp.int32)
    end_of, start_of, owner = lax.fori_loop(0, leafs, spans, (blank, blank, blank))
    my_start = start_sm[me]
    row_id = lax.broadcasted_iota(jnp.int32, (node_total, node_total), 0)
    col_id = lax.broadcasted_iota(jnp.int32, (node_total, node_total), 1)
    mask = mask_ref[...]
    foreign = (mask > 0) & (row_id >= end_of[0:1, :])
    seen = jnp.max(jnp.where(foreign, 1.0, 0.0), axis=0, keepdims=True)
    earlier = jnp.where((row_id < col_id) & (row_id >= start_of[0:1, :]), 1.0, 0.0).astype(jnp.bfloat16)
    seen8 = jnp.broadcast_to(seen, (8, node_total))
    rank8 = jnp.dot(seen8.astype(jnp.bfloat16), earlier, preferred_element_type=jnp.float32)
    owner_f = owner.astype(jnp.float32)
    core_f = lax.rem(owner, 2).astype(jnp.float32)
    chip_f = lax.div(owner, 2).astype(jnp.float32)
    far_place = leafs + core_f * leafs + chip_f * EXPORT + jnp.minimum(rank8, EXPORT - 1.0)
    relative = (lane8 - my_start).astype(jnp.float32)
    place = jnp.where(lane8 >= my_start, relative, far_place)

    slot_row = lax.broadcasted_iota(jnp.int32, (32, node_total), 0)
    slot_col = lax.broadcasted_iota(jnp.int32, (32, node_total), 1)
    own_here = slot_col == my_start + slot_row
    own_mask = jnp.dot(
        jnp.where(own_here, 1.0, 0.0).astype(jnp.bfloat16),
        jnp.where(mask > 0, 1.0, 0.0).astype(jnp.bfloat16),
        preferred_element_type=jnp.float32,
    )
    others = jnp.where((own_mask > 0.5) & ~own_here, 1.0, 0.0)
    before = jnp.where(row_id < col_id, 1.0, 0.0).astype(jnp.bfloat16)
    rank = jnp.dot(others.astype(jnp.bfloat16), before, preferred_element_type=jnp.float32)
    lane32 = lax.broadcasted_iota(jnp.int32, (32, 128), 1)
    row32 = lax.broadcasted_iota(jnp.int32, (32, 128), 0)
    table = jnp.zeros((32, 128), jnp.float32)
    for r in range(ANC - 1):
        hit = (others > 0.5) & (jnp.abs(rank - float(r)) < 0.5)
        value = jnp.sum(jnp.where(hit, place[0:1, :], 0.0), axis=1, keepdims=True)
        table = jnp.where(lane32 == r, value, table)
    table = jnp.where(lane32 == ANC - 1, jnp.sum(others, axis=1, keepdims=True), table)

    pltpu.make_async_copy(ids_in.at[pl.ds(0, leafs - 1)], ids_in.at[pl.ds(0, leafs - 1)], ids_recv).wait()

    def sources(s, total):
        return total + jnp.where(ids_in[s][0:1, :] == my_start + row32, s.astype(jnp.float32), 0.0)

    source = lax.fori_loop(0, leafs, sources, jnp.zeros((32, 128), jnp.float32))
    table = jnp.where(lane32 == 2 * ANC, source, table)
    mine8 = (lane8 >= my_start) & (owner == me) & (seen8 > 0.5)
    for k in range(EXPORT):
        picked = jnp.sum(
            jnp.where(mine8 & (jnp.abs(rank8 - float(k)) < 0.5), relative, 0.0), axis=1, keepdims=True
        )
        chosen = jnp.sum(
            jnp.where(row32.astype(jnp.float32) == picked[0:1, :], source, 0.0), axis=0, keepdims=True
        )
        table = jnp.where(lane32 == 2 * ANC + 1 + k, chosen, table)
    table_vm[...] = table.astype(jnp.int32)
    to_scalars = pltpu.make_async_copy(table_vm, table_sm, table_sem)
    to_scalars.start()
    to_scalars.wait()

    def find_places(r, carry):
        place_sm[r * ANC] = jnp.clip(table_sm[r, 2 * ANC], 0, leafs - 1)
        for p in range(ANC - 1):
            v = table_sm[r, p]
            near = table_sm[jnp.clip(v, 0, leafs - 1), 2 * ANC]
            place_sm[r * ANC + p + 1] = jnp.clip(jnp.where(v < leafs, near, v), 0, leafs + leafs * EXPORT - 1)
        return carry

    lax.fori_loop(0, SLOTS, find_places, 0)
    my_count = part_ref[me]

    for load in loads:
        load.wait()
    def accumulate(src, c, first):
        wide = pieces[src, c].reshape(rows, feat).astype(jnp.float32)
        gain = gain_vm[src]
        scaled[...] = (wide * gain).astype(jnp.bfloat16)
        part = jnp.sum(wide * wide, axis=1, keepdims=True)
        if first:
            squares[...] = jnp.broadcast_to(part, (rows, 128))
        else:
            squares[...] += jnp.broadcast_to(part, (rows, 128))
        if src is opposite:
            return
        product = jnp.dot(scaled[...], weights[src], preferred_element_type=jnp.float32)
        if first:
            acc[...] = product
        else:
            acc[...] += product

    def slot_copy(step, c):
        peer = chip_at(step[0], step[1]) * 2 + lax.rem(core + step[2], 2)
        return pltpu.make_async_remote_copy(
            src_ref=send.at[c, peer],
            dst_ref=recv.at[c, me],
            send_sem=slot_send.at[c],
            recv_sem=slot_recv.at[c],
            device_id=(peer, z),
            device_id_type=MESH,
        )

    def all_slots(buffer, c, sem):
        part = buffer.at[c, pl.ds(0, leafs - 1)]
        pltpu.make_async_copy(part, part, sem.at[c]).wait()

    place = core * chips + chip

    def chip_copy(step, c):
        part = far.at[c, place]
        return pltpu.make_async_remote_copy(
            src_ref=part, dst_ref=part, send_sem=chip_send.at[c], recv_sem=chip_recv.at[c],
            device_id=(chip_at(step[0], step[1]) * 2 + core, z), device_id_type=MESH,
        )

    def chips_arrived(c):
        part = far.at[c, pl.ds(0, chips - 1)]
        pltpu.make_async_copy(part, part, chip_recv.at[c]).wait()

    def core_copy(c):
        part = far.at[c, pl.ds(core * chips, chips)]
        return pltpu.make_async_remote_copy(
            src_ref=part, dst_ref=part, send_sem=core_send.at[c], recv_sem=core_recv.at[c],
            device_id=(chip * 2 + 1 - core, z), device_id_type=MESH,
        )

    def core_arrival(c):
        part = far.at[c, pl.ds((1 - core) * chips, chips)]
        return pltpu.make_async_remote_copy(
            src_ref=part, dst_ref=part, send_sem=core_send.at[c], recv_sem=core_recv.at[c],
            device_id=(chip * 2 + 1 - core, z), device_id_type=MESH,
        )

    kv_cols = 2 * k_cols

    def export_start(c):
        all_slots(recv, c, slot_recv)

        def keep(i, carry):
            for n in range(4):
                near[i * 4 + n] = recv[c, i * 4 + n]
            return carry

        lax.fori_loop(0, leafs // 4, keep, 0)
        exported = [
            near[jnp.clip(table_sm[0, 2 * ANC + 1 + k], 0, leafs - 1)].astype(jnp.float32)[:SUB]
            for k in range(EXPORT)
        ]
        far[c, place] = jnp.concatenate(exported, axis=0).astype(jnp.bfloat16)
        for step in CHIP_STEPS:
            chip_copy(step, c).start()

    def join(even, odd, k):
        at = slice(k * SUB, (k + 1) * SUB)
        return jnp.concatenate([even[at], odd[at]], axis=0).astype(jnp.bfloat16)

    def gather_near(c):
        def keep(i, carry):
            for n in range(2):
                s = i * 2 + n
                even, odd = recv[2 * c, s].astype(jnp.float32), recv[2 * c + 1, s].astype(jnp.float32)
                pool[c, s] = join(even, odd, 0)
                query[c, s] = join(even, odd, 1)
            return carry

        lax.fori_loop(0, leafs // 2, keep, 0)

    def gather_far(c):
        def keep(i, carry):
            for n in range(2):
                s = i * 2 + n
                even, odd = far[2 * c, s].astype(jnp.float32), far[2 * c + 1, s].astype(jnp.float32)
                for k in range(EXPORT):
                    pool[c, leafs + s * EXPORT + k] = join(even, odd, k)
            return carry

        lax.fori_loop(0, leafs // 2, keep, 0)

    def export_core(c):
        chips_arrived(c)
        core_copy(c).start()

    def export_end(c):
        core_arrival(2 * c).wait_recv()
        core_arrival(2 * c + 1).wait_recv()
        gather_far(c)

    heads = k_cols // HD
    groups = q_cols // k_cols
    q_rows = groups * TOK
    lane = lax.broadcasted_iota(jnp.int32, (1, ANC * TOK), 1)

    tri = lax.broadcasted_iota(jnp.int32, (q_rows, ANC * TOK), 1) <= lax.rem(
        lax.broadcasted_iota(jnp.int32, (q_rows, ANC * TOK), 0), TOK
    )
    tri = tri | (lax.broadcasted_iota(jnp.int32, (q_rows, ANC * TOK), 1) >= TOK)

    def load_queries(own, h, first, last):
        return jnp.concatenate(
            [
                query[c, own, :, pl.ds((h * groups + g) * HD, HD)]
                for c in range(first, last)
                for g in range(groups)
            ],
            axis=0,
        )

    def load_pool(places, column, first, last):
        return jnp.concatenate(
            [pool[c, p, :, pl.ds(column, HD)] for c in range(first, last) for p in places], axis=0
        )

    def attend(q0, q1, k0, k1, final):
        at = pl.ds(q0 * q_rows, (q1 - q0) * q_rows)

        def batch(slots):
            chains = [(n, h) for n in range(len(slots)) for h in range(heads)]
            places = [[place_sm[r * ANC + p] for p in range(ANC)] for r in slots]
            limit = [lane < (table_sm[r, ANC - 1] + 1) * TOK for r in slots]
            past = [x & (lane >= TOK) for x in limit]
            scores = {
                (n, h): lax.dot_general(
                    load_queries(places[n][0], h, q0, q1),
                    load_pool(places[n], h * HD, k0, k1),
                    (((1,), (1,)), ((), ())),
                    preferred_element_type=jnp.float32,
                )
                for n, h in chains
            }
            probs, sums = {}, {}
            for n, h in chains:
                capped = jnp.tanh(scores[n, h] * (query_scale / soft_cap))
                raised = jnp.exp2(capped * (soft_cap * math.log2(math.e)))
                lines, adds = [], []
                for q in range(q0, q1):
                    tiles = []
                    for k in range(k0, k1):
                        tile = raised[
                            (q - q0) * q_rows : (q - q0 + 1) * q_rows,
                            (k - k0) * ANC * TOK : (k - k0 + 1) * ANC * TOK,
                        ]
                        keep = limit[n] if k < q else past[n] if k > q else limit[n] & tri
                        tiles.append(jnp.where(keep, tile, 0.0))
                    lines.append(jnp.concatenate(tiles, axis=1))
                    adds.append(functools.reduce(lambda x, y: x + y, tiles))
                probs[n, h] = jnp.concatenate(lines, axis=0).astype(jnp.bfloat16)
                sums[n, h] = jnp.concatenate(adds, axis=0)
            parts = {
                (n, h): jnp.dot(
                    probs[n, h],
                    load_pool(places[n], k_cols + h * HD, k0, k1),
                    preferred_element_type=jnp.float32,
                )
                for n, h in chains
            }
            if not final:
                for n, h in chains:
                    numer[slots[n], h, at, :] = parts[n, h]
                    total[slots[n], h, at, :] = sums[n, h]
                return
            results = {}
            for n, h in chains:
                whole = jnp.sum(total[slots[n], h] + sums[n, h], axis=1, keepdims=True)
                result = (numer[slots[n], h] + parts[n, h]) * (1.0 / whole)
                results[n, h] = jnp.where(slots[n] < my_count, result, 0.0).astype(jnp.bfloat16)
            for n, h in chains:
                for q in range(CHUNKS):
                    for g in range(groups):
                        start = (q * groups + g) * TOK
                        result_vm[slots[n], pl.ds(q * TOK, TOK), pl.ds((h * groups + g) * HD, HD)] = results[n, h][
                            start : start + TOK
                        ]

        def store(i, size):
            at = pl.ds(i * BATCH, size)
            return pltpu.make_async_copy(result_vm.at[at], out_ref.at[at], out_sem.at[i])

        whole, rest = SLOTS // BATCH, SLOTS % BATCH

        def step(i, carry):
            batch([i * BATCH + n for n in range(BATCH)])
            if final:
                store(i, BATCH).start()
            return carry

        lax.fori_loop(0, whole, step, 0)
        if rest:
            batch(list(range(whole * BATCH, SLOTS)))
        if final:
            if rest:
                store(whole, rest).start()
                store(whole, rest).wait()
            for i in range(whole):
                store(i, BATCH).wait()

    def one_chunk(c, carry):
        accumulate(z, c, True)
        accumulate(left, c, False)
        accumulate(right, c, False)

        for k in range(CHUNKS - 2):

            @pl.when(c == 2 * k + 4)
            def _(k=k):
                gather_near(k)
                export_end(k)

        forward_arrival(0, c).wait_recv()
        forward_arrival(1, c).wait_recv()
        accumulate(opposite, c, False)

        scale = lax.rsqrt(squares[...] / width + norm_epsilon)
        cosine = angle_cos[c]
        sine = angle_sin[c]

        acc[...] += jnp.dot(scaled[...], weights[opposite], preferred_element_type=jnp.float32)

        def head(column):
            value = acc[:, pl.ds(column, HD)] * scale
            if column < q_cols + k_cols:
                value = value * cosine + pltpu.roll(value, HD // 2, 1) * sine
            return value.reshape(nodes, SUB, HD)

        for column in range(0, q_cols, HD):
            both = jnp.concatenate([head(q_cols + column), head(column)], axis=1)
            made[:, :, pl.ds(column, HD)] = both.astype(jnp.bfloat16)

        def fill(i, carry2):
            for n in range(4):
                d = i * 4 + n
                send[c, d] = made[index_sm[d]]
            return carry2

        lax.fori_loop(0, leafs // 4, fill, 0)
        for step in SLOT_STEPS:
            slot_copy(step, c).start()
        recv[c, me] = send[c, me]

        def exports():
            @pl.when(c >= 1)
            def _():
                export_start(c - 1)

            @pl.when(c >= 2)
            def _():
                export_core(c - 2)

        @pl.when(c + 1 < SUBS)
        def _():
            pass_on(c + 1, exports)

        @pl.when(c + 1 == SUBS)
        def _():
            exports()

        return carry

    lax.fori_loop(0, SUBS, one_chunk, 0)

    last = CHUNKS - 1
    gather_near(last - 1)
    export_end(last - 1)
    attend(0, last, 0, last, False)
    export_start(SUBS - 1)
    export_core(SUBS - 2)
    gather_near(last)
    attend(last, CHUNKS, 0, last, False)
    export_core(SUBS - 1)
    export_end(last)
    attend(0, CHUNKS, last, CHUNKS, True)

    def settle(c, carry):
        for side in (0, 1):
            full(side, 0, c).wait_send()
            full(side, 1, c).wait_send()
            forward(side, c).wait_send()
        all_slots(send, c, slot_send)
        exported = far.at[c, pl.ds(0, chips - 1)]
        pltpu.make_async_copy(exported, exported, chip_send.at[c]).wait()
        core_copy(c).wait_send()
        return carry

    lax.fori_loop(0, SUBS, settle, 0)
    pltpu.make_async_copy(ids_out.at[pl.ds(0, leafs - 1)], ids_out.at[pl.ds(0, leafs - 1)], ids_send).wait()


def hand_over(from_ref, to_ref, held, in_sems, out_sems):
    size = -(-SLOTS // OUT_PARTS)
    spans = [pl.ds(i * size, min(size, SLOTS - i * size)) for i in range(OUT_PARTS)]
    loads = [pltpu.make_async_copy(from_ref.at[at], held.at[at], in_sems.at[i]) for i, at in enumerate(spans)]
    stores = [pltpu.make_async_copy(held.at[at], to_ref.at[at], out_sems.at[i]) for i, at in enumerate(spans)]
    for load in loads:
        load.start()
    for load, store in zip(loads, stores):
        load.wait()
        store.start()
    for store in stores:
        store.wait()


def on_device(tokens, norm_gain, w_query, w_key, w_value, gen_node, partition, parent, block_mask):
    leafs = lax.axis_size("leaf")
    nodes = gen_node.shape[0]
    feat = tokens.shape[1]
    width = norm_gain.shape[0]
    q_cols = w_query.shape[1]
    k_cols = w_key.shape[1]
    cols = q_cols + 2 * k_cols
    heads = k_cols // HD
    rows = nodes * SUB
    head_rows = q_cols // k_cols * NODE_TOK
    node_total = parent.shape[0]
    half_dim = HD // 2
    inverse_freq = np.exp(
        np.arange(half_dim, dtype=np.float32) * np.float32(-2.0 * math.log(rope_base) / HD)
    ).astype(np.float32)
    freq = jnp.asarray(np.concatenate([inverse_freq, inverse_freq])[None, :])
    bf16, f32, i32 = jnp.bfloat16, jnp.float32, jnp.int32
    dma = pltpu.SemaphoreType.DMA
    smem = pl.BlockSpec(memory_space=pltpu.SMEM)
    vmem = pl.BlockSpec(memory_space=pltpu.VMEM)
    hbm = pl.BlockSpec(memory_space=pl.ANY)
    out = pl.pallas_call(
        functools.partial(fused_kernel, leafs, nodes, width, q_cols, k_cols),
        out_shape=jax.ShapeDtypeStruct((SLOTS, NODE_TOK, q_cols), bf16),
        in_specs=[smem, smem, smem, vmem, vmem, vmem, hbm, hbm, hbm, hbm],
        out_specs=hbm,
        scratch_shapes=[
            pltpu.VMEM((nodes, NODE_TOK, feat), bf16),
            pltpu.VMEM((4, SUBS, nodes // 2, TOK, feat), bf16),
            pltpu.VMEM((4, feat, cols), bf16),
            pltpu.VMEM((rows, feat), bf16),
            pltpu.VMEM((rows, cols), f32),
            pltpu.VMEM((rows, 128), f32),
            pltpu.VMEM((SUBS, rows, HD), f32),
            pltpu.VMEM((SUBS, rows, HD), f32),
            pltpu.VMEM((nodes, TOK, q_cols), bf16),
            pltpu.VMEM((SUBS, leafs, TOK, q_cols), bf16),
            pltpu.VMEM((SUBS, leafs, TOK, q_cols), bf16),
            pltpu.VMEM((leafs, TOK, q_cols), bf16),
            pltpu.VMEM((SUBS, leafs, TOK, 2 * k_cols), bf16),
            pltpu.VMEM((SLOTS, NODE_TOK, q_cols), bf16),
            pltpu.VMEM((CHUNKS, leafs, TOK, q_cols), bf16),
            pltpu.VMEM((CHUNKS, leafs + leafs * EXPORT, TOK, 2 * k_cols), bf16),
            pltpu.VMEM((SLOTS, heads, head_rows, HD), f32),
            pltpu.VMEM((SLOTS, heads, head_rows, HD), f32),
            pltpu.VMEM((leafs, 8, 128), i32),
            pltpu.VMEM((leafs, 8, 128), i32),
            pltpu.VMEM((32, 128), i32),
            pltpu.VMEM((4, 1, feat), f32),
            pltpu.SMEM((node_total,), i32),
            pltpu.SMEM((leafs,), i32),
            pltpu.SMEM((leafs,), i32),
            pltpu.SMEM((leafs,), i32),
            pltpu.SMEM((32, 128), i32),
            pltpu.SMEM((SLOTS * ANC,), i32),
            dma((-(-SLOTS // BATCH),)),
            dma((3,)),
            dma((CHUNKS,)),
            dma((2, 2, SUBS)),
            dma((2, 2, SUBS)),
            dma((2, SUBS)),
            dma((2, SUBS)),
            dma,
            dma,
            dma,
            dma((SUBS,)),
            dma((SUBS,)),
            dma((SUBS,)),
            dma((SUBS,)),
            dma((SUBS,)),
            dma((SUBS,)),
        ],
        compiler_params=pltpu.CompilerParams(
            collective_id=0, has_side_effects=True, vmem_limit_bytes=62 * 1024 * 1024
        ),
        cost_estimate=pl.CostEstimate(
            flops=2 * nodes * NODE_TOK * width * cols, bytes_accessed=30_000_000, transcendentals=0
        ),
        name="tree_attention",
    )(
        gen_node, partition, parent, block_mask, norm_gain, freq,
        tokens.reshape(nodes, NODE_TOK, feat),
        w_query.reshape(4, feat, q_cols), w_key.reshape(4, feat, k_cols), w_value.reshape(4, feat, k_cols),
    )
    return pl.pallas_call(
        hand_over,
        out_shape=jax.ShapeDtypeStruct((SLOTS, NODE_TOK, q_cols), bf16),
        in_specs=[hbm],
        out_specs=hbm,
        scratch_shapes=[pltpu.VMEM((SLOTS, NODE_TOK, q_cols), bf16), dma((OUT_PARTS,)), dma((OUT_PARTS,))],
        name="hand_over",
    )(out).reshape(CAP * NODE_TOK, q_cols)


def solution(mesh):
    in_specs = (
        P("leaf", "mp"),
        P(),
        P(None, "mp"),
        P(None, "mp"),
        P(None, "mp"),
        P("leaf"),
        P(),
        P(),
        P(),
    )
    out_specs = P("leaf", "mp")
    return jax.shard_map(
        on_device, mesh=mesh, in_specs=in_specs, out_specs=out_specs, check_vma=False
    )
```
